256 devices in a mesh: dp: 32 (over y, x, core), expert: 8 (over z).
Axes of the slice: x: 4, y: 4, z: 8, core: 2. Of those that a mesh axis runs over, the one named last changes fastest.
Arguments:
- tokens: bfloat16 [32768, 1024], P(('dp', 'expert')), may hold values from -24 to 24
- out_grad: bfloat16 [32768, 1024], P(('dp', 'expert')), may hold values from -6 to 6
- expert_ids: int32 [32768, 8], P(('dp', 'expert')), may hold values from 0 to 63, all different within a row; in each aligned block of 128 rows (0 to 127, 128 to 255, ...) at most 20 rows name the same one
- gate_values: bfloat16 [32768, 8], P(('dp', 'expert')), may hold values from 0.049804688 to 1
- gate_weight: bfloat16 [1024, 64, 384], P('dp', 'expert'), may hold values from -0.1875 to 0.1875
- down_weight: bfloat16 [1024, 64, 384], P('dp', 'expert'), may hold values from -0.3125 to 0.3125
Outputs:
- input_grad: bfloat16 [32768, 1024], P(('dp', 'expert'))
- gate_grad: float32 [1024, 64, 384], P('dp', 'expert')
- down_grad: float32 [1024, 64, 384], P('dp', 'expert')
The draws below stay inside these ranges and needn't reach their ends.
Inputs may be any that keep to these rules, and one draw needn't show every extreme that they name: `expert_ids`: each row names 8 different experts. Within the rows of one device (aligned blocks of 128 rows) no expert is named more than 20 times, a bound that some block reaches.
All inputs are finite; a program needn't handle non-finite values.
Results may differ from the reference program's by a relative error of at most 0.018.
Values may be sent and summed in bfloat16 or wider, within the bound.
No kernel may reach another device: no remote copies, remote signals or barrier semaphores. Data moves between devices by JAX's collectives and lax.ppermute only.
A program may use at most 128 MiB of HBM per device.

```python
import math
import jax
import jax.numpy as jnp
import numpy as np
from jax import lax

D = 1024
H = 384
TOPK = 8
TOK_DEV = 128
EXPERTS = 64
TOKENS = 32768
CAP = 20
N_DP = 32
N_EXPERT = 8


def with_spikes(result, own_key, source, target, shards_of, factor):
    def block_of(dim):
        return (jnp.arange(result.shape[dim]) // (result.shape[dim] // shards_of)).reshape((-1,) + (1,) * (result.ndim - 1 - dim))

    near = jax.random.permutation(own_key, shards_of)[block_of(target)]
    second = (block_of(target) + shards_of // 2) % shards_of
    return jnp.where((block_of(source) == near) | (block_of(source) == second), factor * result, result)


def block_levels(rng, dims, split, smallest, top_value):
    def one(position, parts):
        draws = jax.random.uniform(jax.random.fold_in(jax.random.fold_in(rng, 6), position), (parts,), jnp.float32, smallest / len(split), top_value / len(split))
        return jnp.repeat(jnp.exp(draws), dims[position] // parts).reshape((-1,) + (1,) * (len(dims) - position - 1))

    level = one(*split[0])
    for cut in split[1:]:
        level = level * one(*cut)
    return level


def deal_out(stream_key, own, number, rows, count, top, most, skew):
    order = jax.random.permutation(stream_key, count)
    packed, usual = shares(count, rows * top, most, skew, True), shares(count, rows * top, most, skew, False)
    places = jnp.arange(count)

    def named(tallies, offset_by):
        used = int((tallies > 0).sum())
        fixed = max(1, used // 4)
        passed = fixed + (places - fixed + offset_by * (used - fixed)) % max(1, count - fixed)
        return jnp.zeros((count,), jnp.int32).at[order[jnp.where(places < fixed, places, passed)]].set(jnp.asarray(tallies, jnp.int32))

    tallies = jnp.where(number % 4 == 0, named(packed, number // 4), named(usual, number - number // 4 - 1))
    mixed = jax.random.permutation(jax.random.fold_in(own, 3), count)
    source_of, taker = mixed[0:count // 2 * 2:2], mixed[1:count // 2 * 2:2]
    margin = jnp.minimum(tallies[source_of] - 1, most - tallies[taker]) // 2
    margin = jnp.where((source_of == order[0]) | (taker == order[0]) | (tallies[taker] == 0), 0, jnp.maximum(margin, 0))
    passed = jax.random.randint(jax.random.fold_in(own, 4), (count // 2,), 0, 1 << 20) % (margin + 1)
    tallies = tallies.at[source_of].add(-passed).at[taker].add(passed)
    members = jnp.searchsorted(jnp.cumsum(tallies), jnp.arange(rows * top), side="right").astype(jnp.int32)
    grid = members.reshape(top, rows).T
    grid = grid[jax.random.permutation(jax.random.fold_in(own, 1), rows)]
    offset_by = jax.random.randint(jax.random.fold_in(own, 2), (rows, 1), 0, top)
    return jnp.take_along_axis(grid, (jnp.arange(top)[None, :] + offset_by) % top, axis=1)


def shares(number_of, total, bound, lean, full):
    loads = [(1 << 20) // math.isqrt(standing ** lean) + 1 for standing in range(1, number_of + 1)]
    largest = bound if full else min(bound, max(-(-total // number_of), total * loads[0] // sum(loads)))
    least = 1 if total - largest >= number_of - 1 else 0
    holding, rest = [largest] + [least] * (number_of - 1), total - largest - least * (number_of - 1)
    while rest > 0:
        free = [i for i in range(1, number_of) if holding[i] < largest] or [i for i in range(1, number_of) if holding[i] < bound]
        pool, budget = sum([loads[i] for i in free]), rest
        for i in free:
            more = min(bound - holding[i], max(1, budget * loads[i] // pool), rest)
            holding[i] = holding[i] + more
            rest = rest - more
    return np.array(holding)


def centred(key, dims, scale, reach, cuts=(), held_as=jnp.bfloat16):
    factor_of = block_levels(key, dims, cuts, -0.22, 0.18) if cuts else 1.0
    values = jax.random.normal(key, dims, jnp.float32) * scale * factor_of
    return jnp.minimum(jnp.maximum(values, -reach), reach).astype(held_as)


def gaussian_with(key, shape, scale, most, split, heavy, kind=jnp.bfloat16):
    array = scale * jax.random.normal(key, shape, jnp.float32)
    if split:
        array = array * block_levels(key, shape, split, -0.22, 0.18)
    return jnp.clip(with_spikes(array, jax.random.fold_in(key, 3), *heavy), -most, most).astype(kind)


def setup_inputs(seed: int = 0) -> dict:
    arg_keys = jax.random.split(jax.random.key(seed), 7)
    tokens = gaussian_with(arg_keys[0], (TOKENS, D), 1.0, 24.0, ((0, 256),), (0, 1, 256, 6.0))
    out_grad = centred(arg_keys[1], (TOKENS, D), 1.0, 6.0, ((0, 256),))
    expert_ids_keys = jax.random.split(jax.random.fold_in(arg_keys[2], 1), TOKENS // TOK_DEV)
    expert_ids_turns = jax.random.permutation(jax.random.fold_in(arg_keys[2], 3), TOKENS // TOK_DEV)
    expert_ids = jax.vmap(lambda own, number: deal_out(jax.random.fold_in(arg_keys[2], 2), own, number, TOK_DEV, EXPERTS, TOPK, CAP, 2))(expert_ids_keys, expert_ids_turns).reshape((TOKENS, TOPK))
    gate_values = jnp.clip(jnp.exp(math.log(1.0) - 2.9996462 * jax.random.uniform(arg_keys[3], (TOKENS, TOPK), jnp.float32) ** block_levels(arg_keys[3], (TOKENS, TOPK), ((0, 256),), -0.2, 0.2)), 0.049804688, 1.0).astype(jnp.bfloat16)
    gate_weight = centred(arg_keys[4], (D, EXPERTS, H), D ** -0.5, 0.1875, ((0, 32), (1, 8)))
    down_weight = centred(arg_keys[5], (D, EXPERTS, H), H ** -0.5, 0.3125, ((0, 32), (1, 8)))
    return dict(tokens=tokens, out_grad=out_grad, expert_ids=expert_ids, gate_values=gate_values, gate_weight=gate_weight, down_weight=down_weight)


def silu_parts(pre_value):
    sigmoid = jax.nn.sigmoid(pre_value)
    return (pre_value * sigmoid, sigmoid * (1.0 + pre_value * (1.0 - sigmoid)))

def reference(tokens, out_grad, expert_ids, gate_values, gate_weight, down_weight):
    group_rows = TOK_DEV * N_EXPERT
    slot_rows = N_EXPERT * CAP
    grad_scale = 1.0 / math.sqrt(TOKENS * TOPK / EXPERTS)
    token_groups = tokens.reshape(N_DP, group_rows, D)
    cotan_groups = out_grad.reshape(N_DP, group_rows, D)
    id_groups = expert_ids.reshape(N_DP, group_rows, TOPK)
    gate_groups = gate_values.reshape(N_DP, group_rows, TOPK)

    def one_group(totals, group):
        rows_all, grads_all, ids_all, gates_all = group

        def one_expert(input_acc, expert_index):
            hits = ids_all == expert_index
            weighting_all = lax.optimization_barrier(jnp.sum(jnp.where(hits, gates_all.astype(jnp.float32), jnp.float32(0.0)), axis=1))
            chosen = jnp.nonzero(jnp.any(hits, axis=1), size=slot_rows, fill_value=group_rows)[0].astype(jnp.int32)
            safe_rows = jnp.minimum(chosen, group_rows - 1)
            valid = chosen < group_rows
            rows_in = rows_all[safe_rows]
            grads_in = grads_all[safe_rows]
            weighting = jnp.where(valid, weighting_all[safe_rows], jnp.float32(0.0))[:, None]
            w_gate = lax.dynamic_index_in_dim(gate_weight, expert_index, 1, keepdims=False)
            w_down = lax.dynamic_index_in_dim(down_weight, expert_index, 1, keepdims=False)
            pre_value = jnp.dot(rows_in, w_gate, preferred_element_type=jnp.float32)
            active, derivative = silu_parts(pre_value)
            scaled = (weighting * active).astype(jnp.bfloat16)
            hidden_grad = weighting * jnp.dot(grads_in, w_down, preferred_element_type=jnp.float32)
            pre_grad = (hidden_grad * derivative).astype(jnp.bfloat16)
            slot_grad = jnp.dot(pre_grad, w_gate.T, preferred_element_type=jnp.float32).astype(jnp.bfloat16)
            gate_term = (jnp.dot(rows_in.T, pre_grad, preferred_element_type=jnp.float32) * grad_scale).astype(jnp.bfloat16)
            down_term = (jnp.dot(grads_in.T, scaled, preferred_element_type=jnp.float32) * grad_scale).astype(jnp.bfloat16)
            input_acc = input_acc.at[chosen].add(slot_grad.astype(jnp.float32), mode='drop')
            return (input_acc, (gate_term, down_term))
        input_acc, terms = lax.scan(one_expert, jnp.zeros((group_rows, D), jnp.float32), jnp.arange(EXPERTS, dtype=jnp.int32))
        gate_total = totals[0] + jnp.transpose(terms[0].astype(jnp.float32), (1, 0, 2))
        down_total = totals[1] + jnp.transpose(terms[1].astype(jnp.float32), (1, 0, 2))
        return ((gate_total, down_total), input_acc.astype(jnp.bfloat16))
    start_totals = (jnp.zeros((D, EXPERTS, H), jnp.float32), jnp.zeros((D, EXPERTS, H), jnp.float32))
    totals, input_groups = lax.scan(one_group, start_totals, (token_groups, cotan_groups, id_groups, gate_groups))
    return (input_groups.reshape(TOKENS, D), totals[0], totals[1])
```

```python
import math

import jax
import jax.numpy as jnp
from jax import lax
from jax.experimental import pallas as pl
from jax.experimental.pallas import tpu as pltpu
from jax.sharding import Mesh
from jax.sharding import PartitionSpec as P

BF, F32 = jnp.bfloat16, jnp.float32
NY, NX, NC, NZ = 4, 4, 2, 8
ROWS, WIDTH, HID = 128, 1024, 384
EXPERTS_CORE = 4
META = 128
CAP = 20
QUAD = 4
QROWS = QUAD * ROWS
QSLOTS = QUAD * CAP
QUADS = NC * NZ // QUAD
SLOTS = QUADS * QSLOTS
PIECE = 32
SIZES = {"y": NY, "x": NX, "c": NC, "z": NZ}


def shift(value, axis, by):
    n = SIZES[axis]
    return lax.ppermute(value, axis, [(i, (i + by) % n) for i in range(n)])


def dot(a, b, contract):
    return lax.dot_general(a, b, ((contract[:1], contract[1:]), ((), ())), preferred_element_type=F32)


def row_of(pos, ky, kx, rc):
    y, x, c = (pos[0] + ky) % NY, (pos[1] + kx) % NX, (pos[2] + rc) % NC
    return pl.multiple_of(((y * NX + x) * NC + c) * PIECE, PIECE)


def kernel(scale, pos, x_own, x_sis, g_own, g_sis, *refs):
    a_in, b_in = refs[0:4], refs[4:8]
    in_out = refs[8]
    a_out, b_out = refs[9:13], refs[13:17]
    acc, wg, wd, xg, gg, srow, gcol, term = refs[17:]
    e = pl.program_id(0)
    lanes = lax.broadcasted_iota(jnp.int32, (1, META), 1)

    def quad(own, sis, q, columns):
        src = own if q < QUADS // 2 else sis
        part = q % (QUADS // 2)
        block = src[part * QUAD : (part + 1) * QUAD, :, columns]
        return block.reshape(QROWS, block.shape[-1])

    @pl.when(e == 0)
    def _():
        acc[...] = jnp.zeros_like(acc)
        lower = (
            lax.broadcasted_iota(jnp.int32, (QROWS, QROWS), 0) > lax.broadcasted_iota(jnp.int32, (QROWS, QROWS), 1)
        ).astype(F32).astype(BF)
        expert = (pos[3] + lanes).astype(F32)
        for q in range(QUADS):
            meta = quad(x_own, x_sis, q, slice(WIDTH, WIDTH + META)).astype(F32)
            member = jnp.zeros((QROWS, META), F32)
            gates = jnp.zeros((QROWS, META), F32)
            for k in range(8):
                hit = meta[:, k : k + 1] == expert
                member = jnp.where(hit, 1.0, member)
                gates = jnp.where(hit, meta[:, 8 + k : 9 + k], gates)
            rank = dot(lower, member.astype(BF), (1, 0))
            slot = jnp.where(member > 0.0, rank, -1.0)
            srow[q] = jnp.transpose(slot)[:8]
            gcol[q] = gates.astype(BF)

    for ky in range(NY):
        for kx in range(NX):
            for rc in range(NC):
                at = pl.ds(row_of(pos, ky, kx, rc), PIECE)
                wg[at, :] = a_in[ky][kx, rc, 0]
                wd[at, :] = b_in[kx][ky, rc, 0]

    slot_iota = lax.broadcasted_iota(jnp.int32, (QSLOTS, QROWS), 0).astype(F32)
    picks, gate_rows = [], []
    for q in range(QUADS):
        pick = (srow[q, pl.ds(e, 1), :] == slot_iota).astype(F32).astype(BF)
        picks.append(pick)
        at = slice(q * QSLOTS, (q + 1) * QSLOTS)
        xg[at, :] = dot(pick, quad(x_own, x_sis, q, slice(0, WIDTH)), (1, 0)).astype(BF)
        gg[at, :] = dot(pick, quad(g_own, g_sis, q, slice(0, WIDTH)), (1, 0)).astype(BF)
        gate_rows.append(jnp.sum(jnp.where(lanes == e, dot(pick, gcol[q], (1, 0)), 0.0), axis=1, keepdims=True))
    weighting = jnp.concatenate(gate_rows, axis=0)
    pre = dot(xg[...], wg[...], (1, 0))
    hidden = dot(gg[...], wd[...], (1, 0))
    sigmoid = jax.nn.sigmoid(pre)
    scaled = (weighting * (pre * sigmoid)).astype(BF)
    pre_grad = (weighting * hidden * (sigmoid * (1.0 + pre * (1.0 - sigmoid)))).astype(BF)
    slot_grad = dot(pre_grad, wg[...], (1, 1)).astype(BF)
    for q in range(QUADS):
        at = slice(q * QROWS, (q + 1) * QROWS)
        acc[at, :] += dot(picks[q], slot_grad[q * QSLOTS : (q + 1) * QSLOTS], (0, 0))
    term[...] = (dot(xg[...], pre_grad, (0, 0)) * scale).astype(BF)
    for ky in range(NY):
        for kx in range(NX):
            for rc in range(NC):
                a_out[ky][kx, rc, 0] = term[pl.ds(row_of(pos, ky, kx, rc), PIECE), :]
    term[...] = (dot(gg[...], scaled, (0, 0)) * scale).astype(BF)
    for ky in range(NY):
        for kx in range(NX):
            for rc in range(NC):
                b_out[kx][ky, rc, 0] = term[pl.ds(row_of(pos, ky, kx, rc), PIECE), :]

    @pl.when(e == EXPERTS_CORE - 1)
    def _():
        in_out[...] = acc[...].astype(BF).reshape(NC, NZ, ROWS, WIDTH)


def experts(scale, pos, x_own, x_sis, g_own, g_sis, a_in, b_in):
    whole = lambda a: pl.BlockSpec(a.shape, lambda e, p: (0,) * a.ndim, pipeline_mode=pl.Buffered(1))
    piece = pl.BlockSpec((4, NC, 1, PIECE, HID), lambda e, p: (0, 0, e, 0, 0))
    grads = jax.ShapeDtypeStruct((4, NC, EXPERTS_CORE, PIECE, HID), BF)
    in_shape = (NC, NZ, ROWS, WIDTH)
    out = pl.pallas_call(
        lambda *refs: kernel(scale, *refs),
        grid_spec=pltpu.PrefetchScalarGridSpec(
            num_scalar_prefetch=1,
            grid=(EXPERTS_CORE,),
            in_specs=[whole(a) for a in (x_own, x_sis, g_own, g_sis)] + [piece] * 8,
            out_specs=[pl.BlockSpec(in_shape, lambda e, p: (0, 0, 0, 0))] + [piece] * 8,
            scratch_shapes=[
                pltpu.VMEM((NC * NZ * ROWS, WIDTH), F32),
                pltpu.VMEM((WIDTH, HID), BF),
                pltpu.VMEM((WIDTH, HID), BF),
                pltpu.VMEM((SLOTS, WIDTH), BF),
                pltpu.VMEM((SLOTS, WIDTH), BF),
                pltpu.VMEM((QUADS, 8, QROWS), F32),
                pltpu.VMEM((QUADS, QROWS, META), BF),
                pltpu.VMEM((WIDTH, HID), BF),
            ],
        ),
        out_shape=[jax.ShapeDtypeStruct(in_shape, BF)] + [grads] * 8,
        compiler_params=pltpu.CompilerParams(vmem_limit_bytes=58 * 2**20),
        cost_estimate=pl.CostEstimate(flops=12_000_000_000, bytes_accessed=30_000_000, transcendentals=2_000_000),
    )(pos, x_own, x_sis, g_own, g_sis, *a_in, *b_in)
    return out[0], out[1:5], out[5:9]


def gather_plane(own, first, second):
    n1, n2 = SIZES[first], SIZES[second]
    line = jnp.stack([own] + [shift(own, first, -k) for k in range(1, n1)])
    return [line] + [shift(line, second, -k) for k in range(1, n2)]


def scatter_plane(parts, first, second):
    add = lambda arrays: sum(a.astype(F32) for a in arrays)
    line = add([parts[0]] + [shift(parts[k], second, k) for k in range(1, SIZES[second])]).astype(BF)
    return add([line[0]] + [shift(line[k], first, k) for k in range(1, SIZES[first])])


def gather_ring(own, more_left):
    up, down = [own], [own]
    n_up = NZ // 2 if more_left else NZ // 2 - 1
    for _ in range(n_up):
        up.append(shift(up[-1], "z", -1))
    for _ in range(NZ - 1 - n_up):
        down.append(shift(down[-1], "z", 1))
    return jnp.stack(up + down[:0:-1])


def scatter_ring(parts):
    half = NZ // 2
    right, left = parts[half], parts[half + 1]
    for k in range(half - 1, 0, -1):
        right = (parts[k].astype(F32) + shift(right, "z", 1).astype(F32)).astype(BF)
    for k in range(half + 2, NZ):
        left = (parts[k].astype(F32) + shift(left, "z", -1).astype(F32)).astype(BF)
    return parts[0].astype(F32) + shift(right, "z", 1).astype(F32) + shift(left, "z", -1).astype(F32)


def shards(tokens, out_grad, expert_ids, gate_values, gate_weight, down_weight):
    scale = 1.0 / math.sqrt(NY * NX * NC * NZ * ROWS * 8 / 64)
    y, x, c, z = (lax.axis_index(a) for a in ("y", "x", "c", "z"))
    pos = jnp.stack([y, x, c, (z * NC + c) * EXPERTS_CORE]).astype(jnp.int32)
    meta = jnp.concatenate([expert_ids.astype(BF), gate_values], axis=1)
    t_own = jnp.concatenate([tokens, jnp.pad(meta, ((0, 0), (0, META - 16)))], axis=1)

    def mine(weight):
        halves = weight.transpose(1, 0, 2).reshape(NC, EXPERTS_CORE, PIECE, HID)
        keep = jnp.where(c == 0, halves[0], halves[1])
        send = jnp.where(c == 0, halves[1], halves[0])
        return keep, send

    (keep_a, send_a), (keep_b, send_b) = mine(gate_weight), mine(down_weight)
    got = shift(jnp.stack([send_a, send_b]), "c", 1)
    a_in = gather_plane(jnp.stack([keep_a, got[0]]), "x", "y")
    b_in = gather_plane(jnp.stack([keep_b, got[1]]), "y", "x")

    t_all = gather_ring(t_own, True)
    g_all = gather_ring(out_grad, False)
    t_sis = shift(t_all, "c", 1)
    g_sis = shift(g_all, "c", 1)

    in_part, a_out, b_out = experts(scale, pos, t_all, t_sis, g_all, g_sis, a_in, b_in)

    in_sis = shift(in_part[1], "c", 1)
    both = (in_part[0].astype(F32) + in_sis.astype(F32)).astype(BF)
    input_grad = scatter_ring([both[k] for k in range(NZ)]).astype(BF)

    a_sum = scatter_plane(a_out, "x", "y").astype(BF)
    b_sum = scatter_plane(b_out, "y", "x").astype(BF)
    back = shift(jnp.stack([a_sum[1], b_sum[1]]), "c", 1)

    def placed(own, sis):
        both = jnp.where(c == 0, jnp.concatenate([own, sis]), jnp.concatenate([sis, own]))
        return both.transpose(1, 0, 2).astype(F32)

    return input_grad, placed(a_sum[0], back[0]), placed(b_sum[0], back[1])


def solution(mesh):
    fine = Mesh(mesh.devices.reshape(NY, NX, NC, NZ), ("y", "x", "c", "z"))
    rows = P(("y", "x", "c", "z"), None)
    weights = P(("y", "x", "c"), "z", None)
    return jax.shard_map(
        shards,
        mesh=fine,
        in_specs=(rows, rows, rows, rows, weights, weights),
        out_specs=(rows, weights, weights),
        check_vma=False,
    )
```

```python
import math

import jax
import jax.numpy as jnp
from jax import lax
from jax.experimental import pallas as pl
from jax.experimental.pallas import tpu as pltpu
from jax.sharding import Mesh
from jax.sharding import PartitionSpec as P

BF, F32 = jnp.bfloat16, jnp.float32
NY, NX, NC, NZ = 4, 4, 2, 8
ROWS, WIDTH, HID = 128, 1024, 384
EXPERTS_CORE = 4
META = 16
CAP = 20
QROWS = 4 * ROWS
QSLOTS = 4 * CAP
QUADS = NC * NZ * ROWS // QROWS
SLOTS = QUADS * QSLOTS
PIECE = WIDTH // (NY * NX)
SIZES = {"y": NY, "x": NX}
ANYWHERE = pl.BlockSpec(memory_space=pl.ANY)
PARAMS = pltpu.CompilerParams(vmem_limit_bytes=60 * 2**20)


def swap(value):
    return lax.ppermute(value, "c", [(0, 1), (1, 0)])


def step(value, axis, by=1):
    n = SIZES[axis]
    pairs = [(2 * i + c, 2 * ((i + by * (1 - 2 * c)) % n) + c) for i in range(n) for c in range(NC)]
    return lax.ppermute(value, (axis, "c"), pairs)


def shift(value, axis, by):
    n = SIZES[axis]
    return lax.ppermute(value, axis, [(i, (i + by) % n) for i in range(n)])


def dot(a, b, contract):
    return lax.dot_general(a, b, ((contract[:1], contract[1:]), ((), ())), preferred_element_type=F32)


def cost(flops, moved, other=0):
    return pl.CostEstimate(flops=flops, bytes_accessed=moved, transcendentals=other)


def row_of(pos, ky, kx):
    y, x = (pos[0] + ky) & (NY - 1), (pos[1] + kx) & (NX - 1)
    return pl.multiple_of((y * NX + x) * PIECE, PIECE)


def pick_rows(srow):
    iota = lax.broadcasted_iota(jnp.int32, (QSLOTS, QROWS), 0).astype(F32)
    picks = [(srow[e : e + 1, :] == iota).astype(F32).astype(BF) for e in range(EXPERTS_CORE)]
    return jnp.concatenate(picks, axis=0)


def layer_kernel(scale, pos, rows, *refs):
    a_in, b_in = refs[0:4], refs[4:8]
    sums, a_out, b_out = refs[8:10], refs[10:15], refs[15:20]
    wg, wd, term, xg, gg, weighting, slot_grad, srow, before = refs[20:]
    step_id = pl.program_id(0)

    @pl.when(step_id == 0)
    def _():
        token = lambda dim: lax.broadcasted_iota(jnp.int32, (QROWS, QROWS), dim)
        before[...] = (token(0) < token(1)).astype(F32).astype(BF)

    @pl.when(step_id < QUADS)
    def _():
        expert = (pos[3] + lax.broadcasted_iota(jnp.int32, (8, 1), 0)).astype(F32)
        meta = [rows[i * ROWS : i * ROWS + META, 2 * WIDTH :].astype(F32) for i in range(QROWS // ROWS)]
        meta = jnp.concatenate(meta, axis=1)
        member = jnp.zeros((8, QROWS), F32)
        gates = jnp.zeros((8, QROWS), F32)
        for k in range(8):
            hit = meta[k : k + 1, :] == expert
            member = jnp.where(hit, 1.0, member)
            gates = jnp.where(hit, meta[8 + k : 9 + k, :], gates)
        slot = jnp.where(member > 0.0, dot(member.astype(BF), before[...], (1, 0)), -1.0)
        srow[step_id] = slot
        picks = pick_rows(slot)
        at = pl.ds(pl.multiple_of(step_id * QSLOTS, QSLOTS), QSLOTS)
        for half, to in enumerate((xg, gg)):
            to[:, at, :] = (
                dot(picks, rows[:, half * WIDTH : (half + 1) * WIDTH], (1, 0))
                .astype(BF)
                .reshape(EXPERTS_CORE, QSLOTS, WIDTH)
            )
        slot_gates = dot(picks, gates.astype(BF), (1, 1))
        for e in range(EXPERTS_CORE):
            weighting[e, at, :] = jnp.broadcast_to(
                slot_gates[e * QSLOTS : (e + 1) * QSLOTS, e : e + 1], (QSLOTS, 128)
            )

    @pl.when(step_id >= QUADS)
    def _():
        expert_step(scale, pos, step_id - QUADS, a_in, b_in, a_out, b_out, wg, wd, term, xg, gg, weighting, slot_grad)

    @pl.when(step_id == QUADS + EXPERTS_CORE - 1)
    def _():
        half = QUADS // 2
        for other, out in enumerate(sums):
            for i in range(half):
                q = (pos[2] ^ other) * half + i
                total = dot(pick_rows(srow[q]), slot_grad[q], (0, 0))
                out[i * QROWS : (i + 1) * QROWS, :] = total.astype(BF)


def expert_step(scale, pos, e, a_in, b_in, a_out, b_out, wg, wd, term, xg, gg, weighting, slot_grad):
    way = pos[4]
    for ky in range(NY):
        for kx in range(NX):
            at = pl.ds(row_of(pos, -way * ky, -way * kx), PIECE)
            wg[at, :] = a_in[ky][kx, 0]
            wd[at, :] = b_in[kx][ky, 0]
    gate = weighting[e][:, :1]
    pre = dot(xg[e], wg[...], (1, 0))
    hidden = dot(gg[e], wd[...], (1, 0))
    sigmoid = jax.nn.sigmoid(pre)
    scaled = (gate * (pre * sigmoid)).astype(BF)
    grad = (gate * hidden * (sigmoid * (1.0 + pre * (1.0 - sigmoid)))).astype(BF)
    back = dot(grad, wg[...], (1, 1)).astype(BF)
    for q in range(QUADS):
        slot_grad[q, pl.ds(pl.multiple_of(e * QSLOTS, QSLOTS), QSLOTS), :] = back[q * QSLOTS : (q + 1) * QSLOTS]
    for rows, value, out, y_first in ((xg, grad, a_out, True), (gg, scaled, b_out, False)):
        term[...] = (dot(rows[e], value, (0, 0)) * scale).astype(BF)
        for k in range(4):
            for j in range(4):
                piece = term[pl.ds(row_of(pos, *((k, j) if y_first else (j, k))), PIECE), :]
                if k == 2:
                    out[2 + j // 2][j % 2, 0] = piece
                else:
                    out[4 if k == 3 else k][j, 0] = piece


def layer(scale, pos, rows, a_in, b_in):
    expert = lambda i: jnp.maximum(i - QUADS, 0)
    piece = lambda n: pl.BlockSpec((n, 1, PIECE, HID), lambda i, p: (0, expert(i), 0, 0))
    grads = lambda n: jax.ShapeDtypeStruct((n, EXPERTS_CORE, PIECE, HID), BF)
    half = (QUADS * QROWS // 2, WIDTH)
    sizes = (4, 4, 2, 2, 4) * 2
    slots = lambda n, dtype: pltpu.VMEM((EXPERTS_CORE, SLOTS, n), dtype)
    out = pl.pallas_call(
        lambda *refs: layer_kernel(scale, *refs),
        grid_spec=pltpu.PrefetchScalarGridSpec(
            num_scalar_prefetch=1,
            grid=(QUADS + EXPERTS_CORE,),
            in_specs=[pl.BlockSpec((QROWS, rows.shape[1]), lambda i, p: (jnp.minimum(i, QUADS - 1), 0))]
            + [piece(4)] * 8,
            out_specs=[pl.BlockSpec(half, lambda i, p: (0, 0))] * 2 + [piece(n) for n in sizes],
            scratch_shapes=[pltpu.VMEM((WIDTH, HID), BF)] * 3
            + [slots(WIDTH, BF), slots(WIDTH, BF), slots(128, F32)]
            + [pltpu.VMEM((QUADS, EXPERTS_CORE * QSLOTS, WIDTH), BF), pltpu.VMEM((QUADS, 8, QROWS), F32)]
            + [pltpu.VMEM((QROWS, QROWS), BF)],
        ),
        out_shape=[jax.ShapeDtypeStruct(half, BF)] * 2 + [grads(n) for n in sizes],
        compiler_params=PARAMS,
        cost_estimate=cost(13_000_000_000, 26_000_000, 600_000),
    )(pos, rows, *a_in, *b_in)
    return out[0], out[1], out[2:7], out[7:12]


def add_kernel(own, got, *refs):
    refs[-1][...] = (own[...].astype(F32) + got[...].astype(F32)).astype(BF)


def add(own, got, after):
    rows = pl.BlockSpec((QROWS // 2, WIDTH), lambda i: (i, 0))
    return pl.pallas_call(
        add_kernel,
        grid=(own.shape[0] * 2 // QROWS,),
        in_specs=[rows, rows] + [ANYWHERE] * len(after),
        out_specs=rows,
        out_shape=jax.ShapeDtypeStruct(own.shape, BF),
        compiler_params=PARAMS,
        cost_estimate=cost(1_000_000, 6_000_000),
    )(own, got, *after)


def gather_plane(own, first, second):
    plane = [jnp.stack([own] + [step(own, first, k) for k in range(1, SIZES[first])])]
    for _ in range(SIZES[second] - 1):
        plane.append(step(plane[-1], second))
    return plane


def passed_on(after, before, up, down):
    f32 = lambda a: a.astype(F32)
    n = up.shape[0]
    return (
        after.at[:n].set((f32(after[:n]) + f32(up)).astype(BF)),
        before.at[n:].set((f32(before[n:]) + f32(down)).astype(BF)),
    )


def scatter_line(own, after, before, axis):
    f32 = lambda a: a.astype(F32)
    return (f32(own) + f32(shift(after, axis, 1)) + f32(shift(before, axis, -1))).astype(BF)


def scatter_last(line, axis):
    return sum([line[0].astype(F32)] + [shift(line[k], axis, k).astype(F32) for k in range(1, SIZES[axis])])


def shards(tokens, out_grad, expert_ids, gate_values, gate_weight, down_weight):
    scale = 1.0 / math.sqrt(NY * NX * NC * NZ * ROWS * 8 / 64)
    y, x, c, z = (lax.axis_index(a) for a in ("y", "x", "c", "z"))
    pos = jnp.stack([y, x, c, (z * NC + c) * EXPERTS_CORE, 1 - 2 * c]).astype(jnp.int32)
    meta = jnp.concatenate([expert_ids.T.astype(BF), gate_values.T], axis=0)
    meta = jnp.pad(meta, ((0, ROWS - META), (0, 0)))
    rows = lax.all_gather(jnp.concatenate([tokens, out_grad, meta], axis=1), ("c", "z"), axis=0, tiled=True)

    def by_core(own, sister):
        return jnp.where(c == 0, own, sister), jnp.where(c == 0, sister, own)

    def halves(weight):
        rows = weight.transpose(1, 0, 2).reshape(NC, EXPERTS_CORE, weight.shape[0], HID)
        return by_core(rows[0], rows[1])

    (keep_a, send_a), (keep_b, send_b) = halves(gate_weight), halves(down_weight)
    got = swap(jnp.stack([send_a, send_b]))
    own_a = jnp.concatenate(by_core(keep_a, got[0]), axis=1)
    own_b = jnp.concatenate(by_core(keep_b, got[1]), axis=1)
    a_in = gather_plane(own_a, "x", "y")
    b_in = gather_plane(own_b, "y", "x")
    own, sister, a_out, b_out = layer(scale, pos, rows, a_in, b_in)
    a_up, a_down = shift(a_out[2], "y", 1), shift(a_out[3], "y", -1)
    b_up, b_down = shift(b_out[2], "x", 1), shift(b_out[3], "x", -1)
    a_ends = passed_on(a_out[1], a_out[4], a_up, a_down)
    b_ends = passed_on(b_out[1], b_out[4], b_up, b_down)
    partial = add(own, swap(sister), (*a_ends, *b_ends))
    input_grad = lax.psum_scatter(partial, "z", scatter_dimension=0, tiled=True)
    a_line = scatter_line(a_out[0], *a_ends, "y")
    b_line = scatter_line(b_out[0], *b_ends, "x")

    sums = jnp.stack([scatter_last(a_line, "x"), scatter_last(b_line, "y")]).astype(BF)
    n = gate_weight.shape[0]
    keep, send = by_core(sums[:, :, :n], sums[:, :, n:])
    back = swap(send)

    def placed(k):
        return jnp.concatenate(by_core(keep[k], back[k])).transpose(1, 0, 2).astype(F32)

    return input_grad, placed(0), placed(1)


def solution(mesh):
    fine = Mesh(mesh.devices.reshape(NY, NX, NC, NZ), ("y", "x", "c", "z"))
    rows = P(("y", "x", "c", "z"), None)
    weights = P(("y", "x", "c"), "z", None)
    return jax.shard_map(
        shards,
        mesh=fine,
        in_specs=(rows, rows, rows, rows, weights, weights),
        out_specs=(rows, weights, weights),
        check_vma=False,
    )
```

```python
import math

import jax
import jax.numpy as jnp
from jax import lax
from jax.experimental import pallas as pl
from jax.experimental.pallas import tpu as pltpu
from jax.sharding import Mesh
from jax.sharding import PartitionSpec as P

BF, F32 = jnp.bfloat16, jnp.float32
NY, NX, NC, NZ = 4, 4, 2, 8
ROWS, WIDTH, HID = 128, 1024, 384
EXPERTS_CORE = 4
META = 16
CAP = 20
QROWS = 4 * ROWS
QSLOTS = 4 * CAP
QUADS = NC * NZ * ROWS // QROWS
SLOTS = QUADS * QSLOTS
PIECE = WIDTH // (NY * NX)
PARTS = (4, 4, 4, 2, 2)
SIZES = {"y": NY, "x": NX}
ANYWHERE = pl.BlockSpec(memory_space=pl.ANY)
PARAMS = pltpu.CompilerParams(vmem_limit_bytes=60 * 2**20)


def swap(value):
    return lax.ppermute(value, "c", [(0, 1), (1, 0)])


def step(value, axis, by=1):
    n = SIZES[axis]
    pairs = [(2 * i + c, 2 * ((i + by * (1 - 2 * c)) % n) + c) for i in range(n) for c in range(NC)]
    return lax.ppermute(value, (axis, "c"), pairs)


def shift(value, axis, by):
    n = SIZES[axis]
    return lax.ppermute(value, axis, [(i, (i + by) % n) for i in range(n)])


def dot(a, b, contract):
    return lax.dot_general(a, b, ((contract[:1], contract[1:]), ((), ())), preferred_element_type=F32)


def cost(flops, moved, other=0):
    return pl.CostEstimate(flops=flops, bytes_accessed=moved, transcendentals=other)


def row_of(pos, ky, kx):
    y, x = (pos[0] + ky) & (NY - 1), (pos[1] + kx) & (NX - 1)
    return pl.multiple_of((y * NX + x) * PIECE, PIECE)


def pick_rows(srow):
    iota = lax.broadcasted_iota(jnp.int32, (QSLOTS, QROWS), 0).astype(F32)
    picks = [(srow[e : e + 1, :] == iota).astype(F32).astype(BF) for e in range(EXPERTS_CORE)]
    return jnp.concatenate(picks, axis=0)


def layer_kernel(scale, pos, rows, *refs):
    a_in, b_in = refs[0:4], refs[4:8]
    sums, a_out, b_out = refs[8], refs[9:14], refs[14:19]
    wg, wd, term, xg, gg, weighting, slot_grad, srow, before = refs[19:]
    step_id = pl.program_id(0)

    @pl.when(step_id == 0)
    def _():
        token = lambda dim: lax.broadcasted_iota(jnp.int32, (QROWS, QROWS), dim)
        before[...] = (token(0) < token(1)).astype(F32).astype(BF)

    @pl.when(step_id < QUADS)
    def _():
        expert = (pos[3] + lax.broadcasted_iota(jnp.int32, (8, 1), 0)).astype(F32)
        meta = [rows[i * ROWS : i * ROWS + META, 2 * WIDTH :].astype(F32) for i in range(QROWS // ROWS)]
        meta = jnp.concatenate(meta, axis=1)
        member = jnp.zeros((8, QROWS), F32)
        gates = jnp.zeros((8, QROWS), F32)
        for k in range(8):
            hit = meta[k : k + 1, :] == expert
            member = jnp.where(hit, 1.0, member)
            gates = jnp.where(hit, meta[8 + k : 9 + k, :], gates)
        slot = jnp.where(member > 0.0, dot(member.astype(BF), before[...], (1, 0)), -1.0)
        srow[step_id] = slot
        picks = pick_rows(slot)
        at = pl.ds(pl.multiple_of(step_id * QSLOTS, QSLOTS), QSLOTS)
        for half, to in enumerate((xg, gg)):
            to[:, at, :] = (
                dot(picks, rows[:, half * WIDTH : (half + 1) * WIDTH], (1, 0))
                .astype(BF)
                .reshape(EXPERTS_CORE, QSLOTS, WIDTH)
            )
        slot_gates = dot(picks, gates.astype(BF), (1, 1))
        for e in range(EXPERTS_CORE):
            weighting[e, at, :] = jnp.broadcast_to(
                slot_gates[e * QSLOTS : (e + 1) * QSLOTS, e : e + 1], (QSLOTS, 128)
            )

    @pl.when(step_id >= QUADS)
    def _():
        expert_step(scale, pos, step_id - QUADS, a_in, b_in, a_out, b_out, wg, wd, term, xg, gg, weighting, slot_grad)

    @pl.when(step_id == QUADS + EXPERTS_CORE - 1)
    def _():
        n = QROWS // ROWS
        for q in range(QUADS):
            total = dot(pick_rows(srow[q]), slot_grad[q], (0, 0)).astype(BF)
            z = q * n % NZ
            sums[z : z + n, q * n // NZ] = total.reshape(n, ROWS, WIDTH)


def place(k, j):
    if k == 0:
        return 0, j
    if k == 1:
        return (3, j) if j < 2 else (1, j - 2)
    if k == 2:
        return (1, j + 2) if j < 2 else (2, j)
    return (2, j) if j < 2 else (4, j - 2)


def expert_step(scale, pos, e, a_in, b_in, a_out, b_out, wg, wd, term, xg, gg, weighting, slot_grad):
    way = pos[4]
    for ky in range(NY):
        for kx in range(NX):
            at = pl.ds(row_of(pos, -way * ky, -way * kx), PIECE)
            wg[at, :] = a_in[ky][kx, 0]
            wd[at, :] = b_in[kx][ky, 0]
    gate = weighting[e][:, :1]
    pre = dot(xg[e], wg[...], (1, 0))
    hidden = dot(gg[e], wd[...], (1, 0))
    sigmoid = jax.nn.sigmoid(pre)
    scaled = (gate * (pre * sigmoid)).astype(BF)
    grad = (gate * hidden * (sigmoid * (1.0 + pre * (1.0 - sigmoid)))).astype(BF)
    back = dot(grad, wg[...], (1, 1)).astype(BF)
    for q in range(QUADS):
        slot_grad[q, pl.ds(pl.multiple_of(e * QSLOTS, QSLOTS), QSLOTS), :] = back[q * QSLOTS : (q + 1) * QSLOTS]
    for rows, value, out, y_first in ((xg, grad, a_out, True), (gg, scaled, b_out, False)):
        term[...] = (dot(rows[e], value, (0, 0)) * scale).astype(BF)
        for k in range(4):
            for j in range(4):
                piece = term[pl.ds(row_of(pos, *((k, j) if y_first else (j, k))), PIECE), :]
                to, at = place(k, j)
                out[to][at, 0] = piece


def layer(scale, pos, rows, a_in, b_in):
    expert = lambda i: jnp.maximum(i - QUADS, 0)
    piece = lambda n: pl.BlockSpec((n, 1, PIECE, HID), lambda i, p: (0, expert(i), 0, 0))
    grads = lambda n: jax.ShapeDtypeStruct((n, EXPERTS_CORE, PIECE, HID), BF)
    by_z = (NZ, NC, ROWS, WIDTH)
    slots = lambda n, dtype: pltpu.VMEM((EXPERTS_CORE, SLOTS, n), dtype)
    out = pl.pallas_call(
        lambda *refs: layer_kernel(scale, *refs),
        grid_spec=pltpu.PrefetchScalarGridSpec(
            num_scalar_prefetch=1,
            grid=(QUADS + EXPERTS_CORE,),
            in_specs=[pl.BlockSpec((QROWS, rows.shape[1]), lambda i, p: (jnp.minimum(i, QUADS - 1), 0))]
            + [piece(4)] * 8,
            out_specs=[pl.BlockSpec(by_z, lambda i, p: (0, 0, 0, 0))] + [piece(n) for n in PARTS * 2],
            scratch_shapes=[pltpu.VMEM((WIDTH, HID), BF)] * 3
            + [slots(WIDTH, BF), slots(WIDTH, BF), slots(128, F32)]
            + [pltpu.VMEM((QUADS, EXPERTS_CORE * QSLOTS, WIDTH), BF), pltpu.VMEM((QUADS, 8, QROWS), F32)]
            + [pltpu.VMEM((QROWS, QROWS), BF)],
        ),
        out_shape=[jax.ShapeDtypeStruct(by_z, BF)] + [grads(n) for n in PARTS * 2],
        compiler_params=PARAMS,
        cost_estimate=cost(13_000_000_000, 26_000_000, 600_000),
    )(pos, rows, *a_in, *b_in)
    return out[0], out[1:6], out[6:11]


def gather_plane(own, first, second):
    plane = [jnp.stack([own] + [step(own, first, k) for k in range(1, SIZES[first])])]
    for _ in range(SIZES[second] - 1):
        plane.append(step(plane[-1], second))
    return plane


def scatter_plane(parts, first, second):
    f32 = lambda a: a.astype(F32)
    own, up, down, next_up, next_down = parts
    up, down = shift(up, second, 1), shift(down, second, -1)
    n = own.shape[0] // 2
    next_up = shift((f32(next_up) + f32(up[n:])).astype(BF), second, 1)
    next_down = shift((f32(next_down) + f32(down[n:])).astype(BF), second, -1)
    low = f32(own[:n]) + f32(next_up) + f32(down[:n])
    high = f32(own[n:]) + f32(up[:n]) + f32(next_down)
    line = [half[i] for half in (low, high) for i in range(n)]
    return sum([line[0]] + [f32(shift(line[k].astype(BF), first, k)) for k in range(1, SIZES[first])])


def shards(tokens, out_grad, expert_ids, gate_values, gate_weight, down_weight):
    scale = 1.0 / math.sqrt(NY * NX * NC * NZ * ROWS * 8 / 64)
    y, x, c, z = (lax.axis_index(a) for a in ("y", "x", "c", "z"))
    pos = jnp.stack([y, x, c, (z * NC + c) * EXPERTS_CORE, 1 - 2 * c]).astype(jnp.int32)
    meta = jnp.concatenate([expert_ids.T.astype(BF), gate_values.T], axis=0)
    meta = jnp.pad(meta, ((0, ROWS - META), (0, 0)))
    rows = lax.all_gather(jnp.concatenate([tokens, out_grad, meta], axis=1), ("c", "z"), axis=0, tiled=True)

    def by_core(own, sister):
        return jnp.where(c == 0, own, sister), jnp.where(c == 0, sister, own)

    def halves(weight):
        rows = weight.transpose(1, 0, 2).reshape(NC, EXPERTS_CORE, weight.shape[0], HID)
        return by_core(rows[0], rows[1])

    (keep_a, send_a), (keep_b, send_b) = halves(gate_weight), halves(down_weight)
    got = swap(jnp.stack([send_a, send_b]))
    own_a = jnp.concatenate(by_core(keep_a, got[0]), axis=1)
    own_b = jnp.concatenate(by_core(keep_b, got[1]), axis=1)
    a_in = gather_plane(own_a, "x", "y")
    b_in = gather_plane(own_b, "y", "x")
    sums, a_out, b_out = layer(scale, pos, rows, a_in, b_in)
    keep, send = by_core(*lax.psum_scatter(sums, "z", scatter_dimension=0))
    input_grad = (keep.astype(F32) + swap(send).astype(F32)).astype(BF)

    def placed(total):
        n = gate_weight.shape[0]
        keep, send = by_core(total[:, :n], total[:, n:])
        both = by_core(keep, swap(send.astype(BF)).astype(F32))
        return jnp.concatenate(both).transpose(1, 0, 2)

    return input_grad, placed(scatter_plane(a_out, "x", "y")), placed(scatter_plane(b_out, "y", "x"))


def solution(mesh):
    fine = Mesh(mesh.devices.reshape(NY, NX, NC, NZ), ("y", "x", "c", "z"))
    rows = P(("y", "x", "c", "z"), None)
    weights = P(("y", "x", "c"), "z", None)
    return jax.shard_map(
        shards,
        mesh=fine,
        in_specs=(rows, rows, rows, rows, weights, weights),
        out_specs=(rows, weights, weights),
        check_vma=False,
    )
```

```python
import math

import jax
import jax.numpy as jnp
from jax import lax
from jax.experimental import pallas as pl
from jax.experimental.pallas import tpu as pltpu
from jax.sharding import Mesh
from jax.sharding import PartitionSpec as P

BF, F32 = jnp.bfloat16, jnp.float32
NY, NX, NC, NZ = 4, 4, 2, 8
ROWS, WIDTH, HID = 128, 1024, 384
EXPERTS_CORE = 4
META = 16
CAP = 20
QROWS = 4 * ROWS
QSLOTS = 4 * CAP
QUADS = NC * NZ * ROWS // QROWS
SLOTS = QUADS * QSLOTS
PIECE = WIDTH // (NY * NX)
PARTS = (4, 4, 4, 2, 2)
SIZES = {"y": NY, "x": NX}
ANYWHERE = pl.BlockSpec(memory_space=pl.ANY)
PARAMS = pltpu.CompilerParams(vmem_limit_bytes=60 * 2**20)


def swap(value):
    return lax.ppermute(value, "c", [(0, 1), (1, 0)])


def step(value, axis, by=1):
    n = SIZES[axis]
    pairs = [(2 * i + c, 2 * ((i + by * (1 - 2 * c)) % n) + c) for i in range(n) for c in range(NC)]
    return lax.ppermute(value, (axis, "c"), pairs)


def shift(value, axis, by):
    n = SIZES[axis]
    return lax.ppermute(value, axis, [(i, (i + by) % n) for i in range(n)])


def dot(a, b, contract):
    return lax.dot_general(a, b, ((contract[:1], contract[1:]), ((), ())), preferred_element_type=F32)


def cost(flops, moved, other=0):
    return pl.CostEstimate(flops=flops, bytes_accessed=moved, transcendentals=other)


def row_of(pos, ky, kx):
    y, x = (pos[0] + ky) & (NY - 1), (pos[1] + kx) & (NX - 1)
    return pl.multiple_of((y * NX + x) * PIECE, PIECE)


def pick_rows(srow):
    iota = lax.broadcasted_iota(jnp.int32, (QSLOTS, QROWS), 0).astype(F32)
    picks = [(srow[e : e + 1, :] == iota).astype(F32).astype(BF) for e in range(EXPERTS_CORE)]
    return jnp.concatenate(picks, axis=0)


def pack_kernel(tokens, out_grad, ids, gates, out, meta, sems):
    parts = ((tokens, 0, WIDTH), (out_grad, WIDTH, WIDTH), (meta, 2 * WIDTH, ROWS))
    copies = [
        pltpu.make_async_copy(part, out.at[:, pl.ds(at, n)], sems.at[i]) for i, (part, at, n) in enumerate(parts)
    ]
    copies[0].start()
    copies[1].start()
    both = jnp.concatenate([ids[...].astype(F32), gates[...].astype(F32)], axis=0).astype(BF)
    meta[:META] = both
    meta[META:] = jnp.zeros((ROWS - META, ROWS), BF)
    copies[2].start()
    for copy in copies:
        copy.wait()


def pack(tokens, out_grad, ids, gates):
    return pl.pallas_call(
        pack_kernel,
        in_specs=[ANYWHERE, ANYWHERE, pl.BlockSpec(memory_space=pltpu.VMEM), pl.BlockSpec(memory_space=pltpu.VMEM)],
        out_specs=ANYWHERE,
        out_shape=jax.ShapeDtypeStruct((ROWS, 2 * WIDTH + ROWS), BF),
        scratch_shapes=[pltpu.VMEM((ROWS, ROWS), BF), pltpu.SemaphoreType.DMA((3,))],
        compiler_params=PARAMS,
        cost_estimate=cost(100_000, 1_100_000),
    )(tokens, out_grad, ids, gates)


def layer_kernel(scale, pos, rows, *refs):
    a_in, b_in = refs[0:4], refs[4:8]
    sums, a_out, b_out = refs[8], refs[9:14], refs[14:19]
    wg, wd, term, xg, gg, weighting, slot_grad, srow, before, totals, sems = refs[19:]
    n = QROWS // ROWS
    out_copies = [
        pltpu.make_async_copy(totals.at[q], sums.at[pl.ds(q * n % NZ, n), q * n // NZ], sems.at[q]) for q in range(QUADS)
    ]
    step_id = pl.program_id(0)

    @pl.when(step_id == 0)
    def _():
        token = lambda dim: lax.broadcasted_iota(jnp.int32, (QROWS, QROWS), dim)
        before[...] = (token(0) < token(1)).astype(F32).astype(BF)

    @pl.when(step_id < QUADS)
    def _():
        expert = (pos[3] + lax.broadcasted_iota(jnp.int32, (8, 1), 0)).astype(F32)
        meta = [rows[i * ROWS : i * ROWS + META, 2 * WIDTH :].astype(F32) for i in range(QROWS // ROWS)]
        meta = jnp.concatenate(meta, axis=1)
        member = jnp.zeros((8, QROWS), F32)
        gates = jnp.zeros((8, QROWS), F32)
        for k in range(8):
            hit = meta[k : k + 1, :] == expert
            member = jnp.where(hit, 1.0, member)
            gates = jnp.where(hit, meta[8 + k : 9 + k, :], gates)
        slot = jnp.where(member > 0.0, dot(member.astype(BF), before[...], (1, 0)), -1.0)
        srow[step_id] = slot
        picks = pick_rows(slot)
        at = pl.ds(pl.multiple_of(step_id * QSLOTS, QSLOTS), QSLOTS)
        for half, to in enumerate((xg, gg)):
            to[:, at, :] = (
                dot(picks, rows[:, half * WIDTH : (half + 1) * WIDTH], (1, 0))
                .astype(BF)
                .reshape(EXPERTS_CORE, QSLOTS, WIDTH)
            )
        slot_gates = dot(picks, gates.astype(BF), (1, 1))
        for e in range(EXPERTS_CORE):
            weighting[e, at, :] = jnp.broadcast_to(
                slot_gates[e * QSLOTS : (e + 1) * QSLOTS, e : e + 1], (QSLOTS, 128)
            )

    @pl.when(step_id >= QUADS)
    def _():
        e = step_id - QUADS
        values = expert_step(pos, e, a_in, b_in, wg, wd, xg, gg, weighting, slot_grad)

        @pl.when(e == EXPERTS_CORE - 1)
        def _():
            for q in range(QUADS):
                total = dot(pick_rows(srow[q]), slot_grad[q], (0, 0)).astype(BF)
                totals[q] = total.reshape(n, ROWS, WIDTH)
                out_copies[q].start()

        for rows_in, value, out, y_first in zip((xg, gg), values, (a_out, b_out), (True, False)):
            term[...] = (dot(rows_in[e], value, (0, 0)) * scale).astype(BF)
            for k in range(4):
                for j in range(4):
                    piece = term[pl.ds(row_of(pos, *((k, j) if y_first else (j, k))), PIECE), :]
                    to, at = place(k, j)
                    out[to][at, 0] = piece

    @pl.when(step_id == QUADS + EXPERTS_CORE - 1)
    def _():
        for copy in out_copies:
            copy.wait()


def place(k, j):
    if k == 0:
        return 0, j
    if k == 1:
        return (3, j) if j < 2 else (1, j - 2)
    if k == 2:
        return (1, j + 2) if j < 2 else (2, j)
    return (2, j) if j < 2 else (4, j - 2)


def expert_step(pos, e, a_in, b_in, wg, wd, xg, gg, weighting, slot_grad):
    way = pos[4]
    for ky in range(NY):
        for kx in range(NX):
            at = pl.ds(row_of(pos, -way * ky, -way * kx), PIECE)
            wg[at, :] = a_in[ky][kx, 0]
            wd[at, :] = b_in[kx][ky, 0]
    gate = weighting[e][:, :1]
    pre = dot(xg[e], wg[...], (1, 0))
    hidden = dot(gg[e], wd[...], (1, 0))
    sigmoid = jax.nn.sigmoid(pre)
    scaled = (gate * (pre * sigmoid)).astype(BF)
    grad = (gate * hidden * (sigmoid * (1.0 + pre * (1.0 - sigmoid)))).astype(BF)
    back = dot(grad, wg[...], (1, 1)).astype(BF)
    for q in range(QUADS):
        slot_grad[q, pl.ds(pl.multiple_of(e * QSLOTS, QSLOTS), QSLOTS), :] = back[q * QSLOTS : (q + 1) * QSLOTS]
    return grad, scaled


def layer(scale, pos, rows, a_in, b_in):
    expert = lambda i: jnp.maximum(i - QUADS, 0)
    piece = lambda n: pl.BlockSpec((n, 1, PIECE, HID), lambda i, p: (0, expert(i), 0, 0))
    grads = lambda n: jax.ShapeDtypeStruct((n, EXPERTS_CORE, PIECE, HID), BF)
    by_z = (NZ, NC, ROWS, WIDTH)
    slots = lambda n, dtype: pltpu.VMEM((EXPERTS_CORE, SLOTS, n), dtype)
    out = pl.pallas_call(
        lambda *refs: layer_kernel(scale, *refs),
        grid_spec=pltpu.PrefetchScalarGridSpec(
            num_scalar_prefetch=1,
            grid=(QUADS + EXPERTS_CORE,),
            in_specs=[pl.BlockSpec((QROWS, rows.shape[1]), lambda i, p: (jnp.minimum(i, QUADS - 1), 0))]
            + [piece(4)] * 8,
            out_specs=[ANYWHERE] + [piece(n) for n in PARTS * 2],
            scratch_shapes=[pltpu.VMEM((WIDTH, HID), BF)] * 3
            + [slots(WIDTH, BF), slots(WIDTH, BF), slots(128, F32)]
            + [pltpu.VMEM((QUADS, EXPERTS_CORE * QSLOTS, WIDTH), BF), pltpu.VMEM((QUADS, 8, QROWS), F32)]
            + [pltpu.VMEM((QROWS, QROWS), BF), pltpu.VMEM((QUADS, QROWS // ROWS, ROWS, WIDTH), BF)]
            + [pltpu.SemaphoreType.DMA((QUADS,))],
        ),
        out_shape=[jax.ShapeDtypeStruct(by_z, BF)] + [grads(n) for n in PARTS * 2],
        compiler_params=PARAMS,
        cost_estimate=cost(13_000_000_000, 26_000_000, 600_000),
    )(pos, rows, *a_in, *b_in)
    return out[0], out[1:6], out[6:11]


def gather_plane(own, first, second):
    plane = [jnp.stack([own] + [step(own, first, k) for k in range(1, SIZES[first])])]
    for _ in range(SIZES[second] - 1):
        plane.append(step(plane[-1], second))
    return plane


def scatter_plane(parts, first, second):
    f32 = lambda a: a.astype(F32)
    own, up, down, next_up, next_down = parts
    up, down = shift(up, second, 1), shift(down, second, -1)
    n = own.shape[0] // 2
    next_up = shift((f32(next_up) + f32(up[n:])).astype(BF), second, 1)
    next_down = shift((f32(next_down) + f32(down[n:])).astype(BF), second, -1)
    low = f32(own[:n]) + f32(next_up) + f32(down[:n])
    high = f32(own[n:]) + f32(up[:n]) + f32(next_down)
    line = [half[i] for half in (low, high) for i in range(n)]
    return sum([line[0]] + [f32(shift(line[k].astype(BF), first, k)) for k in range(1, SIZES[first])])


def shards(tokens, out_grad, expert_ids, gate_values, gate_weight, down_weight):
    scale = 1.0 / math.sqrt(NY * NX * NC * NZ * ROWS * 8 / 64)
    y, x, c, z = (lax.axis_index(a) for a in ("y", "x", "c", "z"))
    pos = jnp.stack([y, x, c, (z * NC + c) * EXPERTS_CORE, 1 - 2 * c]).astype(jnp.int32)
    packed = pack(tokens, out_grad, expert_ids.T, gate_values.T)
    rows = lax.all_gather(packed, ("c", "z"), axis=0, tiled=True)

    def by_core(own, sister):
        return jnp.where(c == 0, own, sister), jnp.where(c == 0, sister, own)

    def halves(weight):
        rows = weight.transpose(1, 0, 2).reshape(NC, EXPERTS_CORE, weight.shape[0], HID)
        return by_core(rows[0], rows[1])

    (keep_a, send_a), (keep_b, send_b) = halves(gate_weight), halves(down_weight)
    got = swap(jnp.stack([send_a, send_b]))
    own_a = jnp.concatenate(by_core(keep_a, got[0]), axis=1)
    own_b = jnp.concatenate(by_core(keep_b, got[1]), axis=1)
    a_in = gather_plane(own_a, "x", "y")
    b_in = gather_plane(own_b, "y", "x")
    sums, a_out, b_out = layer(scale, pos, rows, a_in, b_in)
    part = lax.psum_scatter(sums, "z", scatter_dimension=0)
    got = swap(part)
    input_grad = jnp.where(c == 0, part[0].astype(F32) + got[0].astype(F32), part[1].astype(F32) + got[1].astype(F32)).astype(BF)

    def placed(total):
        n = gate_weight.shape[0]
        keep, send = by_core(total[:, :n], total[:, n:])
        both = by_core(keep, swap(send.astype(BF)).astype(F32))
        return jnp.concatenate(both).transpose(1, 0, 2)

    return input_grad, placed(scatter_plane(a_out, "x", "y")), placed(scatter_plane(b_out, "y", "x"))


def solution(mesh):
    fine = Mesh(mesh.devices.reshape(NY, NX, NC, NZ), ("y", "x", "c", "z"))
    rows = P(("y", "x", "c", "z"), None)
    weights = P(("y", "x", "c"), "z", None)
    return jax.shard_map(
        shards,
        mesh=fine,
        in_specs=(rows, rows, rows, rows, weights, weights),
        out_specs=(rows, weights, weights),
        check_vma=False,
    )
```

```python
import math

import jax
import jax.numpy as jnp
from jax import lax
from jax.experimental import pallas as pl
from jax.experimental.pallas import tpu as pltpu
from jax.sharding import Mesh
from jax.sharding import PartitionSpec as P

BF, F32 = jnp.bfloat16, jnp.float32
NY, NX, NC, NZ = 4, 4, 2, 8
ROWS, WIDTH, HID = 128, 1024, 384
EXPERTS_CORE = 4
META = 16
CAP = 20
QROWS = 4 * ROWS
QSLOTS = 4 * CAP
QUADS = NC * NZ * ROWS // QROWS
SLOTS = QUADS * QSLOTS
PIECE = WIDTH // (NY * NX)
PARTS = (4, 4, 4, 2, 2)
SIZES = {"y": NY, "x": NX}
ANYWHERE = pl.BlockSpec(memory_space=pl.ANY)
PARAMS = pltpu.CompilerParams(vmem_limit_bytes=60 * 2**20)


def swap(value):
    return lax.ppermute(value, "c", [(0, 1), (1, 0)])


def step(value, axis, by=1):
    n = SIZES[axis]
    pairs = [(2 * i + c, 2 * ((i + by * (1 - 2 * c)) % n) + c) for i in range(n) for c in range(NC)]
    return lax.ppermute(value, (axis, "c"), pairs)


def shift(value, axis, by):
    n = SIZES[axis]
    return lax.ppermute(value, axis, [(i, (i + by) % n) for i in range(n)])


def dot(a, b, contract):
    return lax.dot_general(a, b, ((contract[:1], contract[1:]), ((), ())), preferred_element_type=F32)


def cost(flops, moved, other=0):
    return pl.CostEstimate(flops=flops, bytes_accessed=moved, transcendentals=other)


def row_of(pos, ky, kx):
    y, x = (pos[0] + ky) & (NY - 1), (pos[1] + kx) & (NX - 1)
    return pl.multiple_of((y * NX + x) * PIECE, PIECE)


def pick_rows(srow):
    iota = lax.broadcasted_iota(jnp.int32, (QSLOTS, QROWS), 0).astype(F32)
    picks = [(srow[e : e + 1, :] == iota).astype(F32).astype(BF) for e in range(EXPERTS_CORE)]
    return jnp.concatenate(picks, axis=0)


def layer_kernel(scale, pos, rows, *refs):
    a_in, b_in = refs[0:4], refs[4:8]
    sums, a_out, b_out = refs[8], refs[9:14], refs[14:19]
    wg, wd, term, xg, gg, weighting, slot_grad, srow, before, totals, sems = refs[19:]
    n = QROWS // ROWS
    out_copies = [
        pltpu.make_async_copy(totals.at[q], sums.at[pl.ds(q * n % NZ, n), q * n // NZ], sems.at[q]) for q in range(QUADS)
    ]
    step_id = pl.program_id(0)

    @pl.when(step_id == 0)
    def _():
        token = lambda dim: lax.broadcasted_iota(jnp.int32, (QROWS, QROWS), dim)
        before[...] = (token(0) < token(1)).astype(F32).astype(BF)

    @pl.when(step_id < QUADS)
    def _():
        expert = (pos[3] + lax.broadcasted_iota(jnp.int32, (8, 1), 0)).astype(F32)
        meta = [rows[i * ROWS : i * ROWS + META, 2 * WIDTH :].astype(F32) for i in range(QROWS // ROWS)]
        meta = jnp.concatenate(meta, axis=1)
        member = jnp.zeros((8, QROWS), F32)
        gates = jnp.zeros((8, QROWS), F32)
        for k in range(8):
            hit = meta[k : k + 1, :] == expert
            member = jnp.where(hit, 1.0, member)
            gates = jnp.where(hit, meta[8 + k : 9 + k, :], gates)
        slot = jnp.where(member > 0.0, dot(member.astype(BF), before[...], (1, 0)), -1.0)
        srow[step_id] = slot
        picks = pick_rows(slot)
        at = pl.ds(pl.multiple_of(step_id * QSLOTS, QSLOTS), QSLOTS)
        for half, to in enumerate((xg, gg)):
            to[:, at, :] = (
                dot(picks, rows[:, half * WIDTH : (half + 1) * WIDTH], (1, 0))
                .astype(BF)
                .reshape(EXPERTS_CORE, QSLOTS, WIDTH)
            )
        slot_gates = dot(picks, gates.astype(BF), (1, 1))
        for e in range(EXPERTS_CORE):
            weighting[e, at, :] = jnp.broadcast_to(
                slot_gates[e * QSLOTS : (e + 1) * QSLOTS, e : e + 1], (QSLOTS, 128)
            )

    @pl.when(step_id >= QUADS)
    def _():
        e = step_id - QUADS
        values = expert_step(pos, e, a_in, b_in, wg, wd, xg, gg, weighting, slot_grad)

        @pl.when(e == EXPERTS_CORE - 1)
        def _():
            for q in range(QUADS):
                total = dot(pick_rows(srow[q]), slot_grad[q], (0, 0)).astype(BF)
                totals[q] = total.reshape(n, ROWS, WIDTH)
                out_copies[q].start()

        for rows_in, value, out, y_first in zip((xg, gg), values, (a_out, b_out), (True, False)):
            term[...] = (dot(rows_in[e], value, (0, 0)) * scale).astype(BF)
            for k in range(4):
                for j in range(4):
                    piece = term[pl.ds(row_of(pos, *((k, j) if y_first else (j, k))), PIECE), :]
                    to, at = place(k, j)
                    out[to][at, 0] = piece

    @pl.when(step_id == QUADS + EXPERTS_CORE - 1)
    def _():
        for copy in out_copies:
            copy.wait()


def place(k, j):
    if k == 0:
        return 0, j
    if k == 1:
        return (3, j) if j < 2 else (1, j - 2)
    if k == 2:
        return (1, j + 2) if j < 2 else (2, j)
    return (2, j) if j < 2 else (4, j - 2)


def expert_step(pos, e, a_in, b_in, wg, wd, xg, gg, weighting, slot_grad):
    way = pos[4]
    for ky in range(NY):
        for kx in range(NX):
            at = pl.ds(row_of(pos, -way * ky, -way * kx), PIECE)
            wg[at, :] = a_in[ky][kx, 0]
            wd[at, :] = b_in[kx][ky, 0]
    gate = weighting[e][:, :1]
    pre = dot(xg[e], wg[...], (1, 0))
    hidden = dot(gg[e], wd[...], (1, 0))
    sigmoid = jax.nn.sigmoid(pre)
    scaled = (gate * (pre * sigmoid)).astype(BF)
    grad = (gate * hidden * (sigmoid * (1.0 + pre * (1.0 - sigmoid)))).astype(BF)
    back = dot(grad, wg[...], (1, 1)).astype(BF)
    for q in range(QUADS):
        slot_grad[q, pl.ds(pl.multiple_of(e * QSLOTS, QSLOTS), QSLOTS), :] = back[q * QSLOTS : (q + 1) * QSLOTS]
    return grad, scaled


def layer(scale, pos, rows, a_in, b_in):
    expert = lambda i: jnp.maximum(i - QUADS, 0)
    piece = lambda n: pl.BlockSpec((n, 1, PIECE, HID), lambda i, p: (0, expert(i), 0, 0))
    grads = lambda n: jax.ShapeDtypeStruct((n, EXPERTS_CORE, PIECE, HID), BF)
    by_z = (NZ, NC, ROWS, WIDTH)
    slots = lambda n, dtype: pltpu.VMEM((EXPERTS_CORE, SLOTS, n), dtype)
    out = pl.pallas_call(
        lambda *refs: layer_kernel(scale, *refs),
        grid_spec=pltpu.PrefetchScalarGridSpec(
            num_scalar_prefetch=1,
            grid=(QUADS + EXPERTS_CORE,),
            in_specs=[pl.BlockSpec((QROWS, rows.shape[1]), lambda i, p: (jnp.minimum(i, QUADS - 1), 0))]
            + [piece(4)] * 8,
            out_specs=[ANYWHERE] + [piece(n) for n in PARTS * 2],
            scratch_shapes=[pltpu.VMEM((WIDTH, HID), BF)] * 3
            + [slots(WIDTH, BF), slots(WIDTH, BF), slots(128, F32)]
            + [pltpu.VMEM((QUADS, EXPERTS_CORE * QSLOTS, WIDTH), BF), pltpu.VMEM((QUADS, 8, QROWS), F32)]
            + [pltpu.VMEM((QROWS, QROWS), BF), pltpu.VMEM((QUADS, QROWS // ROWS, ROWS, WIDTH), BF)]
            + [pltpu.SemaphoreType.DMA((QUADS,))],
        ),
        out_shape=[jax.ShapeDtypeStruct(by_z, BF)] + [grads(n) for n in PARTS * 2],
        compiler_params=PARAMS,
        cost_estimate=cost(13_000_000_000, 26_000_000, 600_000),
    )(pos, rows, *a_in, *b_in)
    return out[0], out[1:6], out[6:11]


def gather_plane(own, first, second):
    plane = [jnp.stack([own] + [step(own, first, k) for k in range(1, SIZES[first])])]
    for _ in range(SIZES[second] - 1):
        plane.append(step(plane[-1], second))
    return plane


def scatter_plane(parts, first, second):
    f32 = lambda a: a.astype(F32)
    own, up, down, next_up, next_down = parts
    up, down = shift(up, second, 1), shift(down, second, -1)
    n = own.shape[0] // 2
    next_up = shift((f32(next_up) + f32(up[n:])).astype(BF), second, 1)
    next_down = shift((f32(next_down) + f32(down[n:])).astype(BF), second, -1)
    low = f32(own[:n]) + f32(next_up) + f32(down[:n])
    high = f32(own[n:]) + f32(up[:n]) + f32(next_down)
    line = [half[i] for half in (low, high) for i in range(n)]
    return sum([line[0]] + [f32(shift(line[k].astype(BF), first, k)) for k in range(1, SIZES[first])])


def shards(tokens, out_grad, expert_ids, gate_values, gate_weight, down_weight):
    scale = 1.0 / math.sqrt(NY * NX * NC * NZ * ROWS * 8 / 64)
    y, x, c, z = (lax.axis_index(a) for a in ("y", "x", "c", "z"))
    pos = jnp.stack([y, x, c, (z * NC + c) * EXPERTS_CORE, 1 - 2 * c]).astype(jnp.int32)
    ids, gates = expert_ids.T.astype(F32), gate_values.T.astype(F32)
    first = jnp.arange(META)[:, None] < META // 2
    meta = jnp.where(first, jnp.concatenate([ids, ids]), jnp.concatenate([gates, gates])).astype(BF)
    meta = jnp.pad(meta, ((0, ROWS - META), (0, 0)))
    rows = lax.all_gather(jnp.concatenate([tokens, out_grad, meta], axis=1), ("c", "z"), axis=0, tiled=True)

    def by_core(own, sister):
        return jnp.where(c == 0, own, sister), jnp.where(c == 0, sister, own)

    def halves(weight):
        rows = weight.transpose(1, 0, 2).reshape(NC, EXPERTS_CORE, weight.shape[0], HID)
        return by_core(rows[0], rows[1])

    (keep_a, send_a), (keep_b, send_b) = halves(gate_weight), halves(down_weight)
    got = swap(jnp.stack([send_a, send_b]))
    own_a = jnp.concatenate(by_core(keep_a, got[0]), axis=1)
    own_b = jnp.concatenate(by_core(keep_b, got[1]), axis=1)
    a_in = gather_plane(own_a, "x", "y")
    b_in = gather_plane(own_b, "y", "x")
    sums, a_out, b_out = layer(scale, pos, rows, a_in, b_in)
    part = lax.psum_scatter(sums, "z", scatter_dimension=0)
    got = swap(part)
    input_grad = jnp.where(c == 0, part[0].astype(F32) + got[0].astype(F32), part[1].astype(F32) + got[1].astype(F32)).astype(BF)

    def placed(total):
        n = gate_weight.shape[0]
        keep, send = by_core(total[:, :n], total[:, n:])
        both = by_core(keep, swap(send.astype(BF)).astype(F32))
        return jnp.concatenate(both).transpose(1, 0, 2)

    return input_grad, placed(scatter_plane(a_out, "x", "y")), placed(scatter_plane(b_out, "y", "x"))


def solution(mesh):
    fine = Mesh(mesh.devices.reshape(NY, NX, NC, NZ), ("y", "x", "c", "z"))
    rows = P(("y", "x", "c", "z"), None)
    weights = P(("y", "x", "c"), "z", None)
    return jax.shard_map(
        shards,
        mesh=fine,
        in_specs=(rows, rows, rows, rows, weights, weights),
        out_specs=(rows, weights, weights),
        check_vma=False,
    )
```

```python
import math

import jax
import jax.numpy as jnp
from jax import lax
from jax.experimental import pallas as pl
from jax.experimental.pallas import tpu as pltpu
from jax.sharding import Mesh
from jax.sharding import PartitionSpec as P

BF, F32 = jnp.bfloat16, jnp.float32
NY, NX, NC, NZ = 4, 4, 2, 8
ROWS, WIDTH, HID = 128, 1024, 384
EXPERTS_CORE = 4
META = 16
CAP = 20
QROWS = 4 * ROWS
QSLOTS = 4 * CAP
QUADS = NC * NZ * ROWS // QROWS
SLOTS = QUADS * QSLOTS
PIECE = WIDTH // (NY * NX)
PARTS = (4, 4, 4, 2, 2)
SIZES = {"y": NY, "x": NX}
ANYWHERE = pl.BlockSpec(memory_space=pl.ANY)
PARAMS = pltpu.CompilerParams(vmem_limit_bytes=54 * 2**20)


def swap(value):
    return lax.ppermute(value, "c", [(0, 1), (1, 0)])


def step(value, axis, by=1):
    n = SIZES[axis]
    pairs = [(2 * i + c, 2 * ((i + by * (1 - 2 * c)) % n) + c) for i in range(n) for c in range(NC)]
    return lax.ppermute(value, (axis, "c"), pairs)


def shift(value, axis, by):
    n = SIZES[axis]
    return lax.ppermute(value, axis, [(i, (i + by) % n) for i in range(n)])


def dot(a, b, contract):
    return lax.dot_general(a, b, ((contract[:1], contract[1:]), ((), ())), preferred_element_type=F32)


def cost(flops, moved, other=0):
    return pl.CostEstimate(flops=flops, bytes_accessed=moved, transcendentals=other)


def row_of(pos, ky, kx):
    y, x = (pos[0] + ky) & (NY - 1), (pos[1] + kx) & (NX - 1)
    return pl.multiple_of((y * NX + x) * PIECE, PIECE)


def pick_rows(srow):
    iota = lax.broadcasted_iota(jnp.int32, (QSLOTS, QROWS), 0).astype(F32)
    picks = [(srow[e : e + 1, :] == iota).astype(F32).astype(BF) for e in range(EXPERTS_CORE)]
    return jnp.concatenate(picks, axis=0)


def layer_kernel(scale, pos, rows, *refs):
    a_in, b_in = refs[0:4], refs[4:8]
    sums, a_out, b_out = refs[8], refs[9:14], refs[14:19]
    wg, wd, term, xg, gg, weighting, slot_grad, srow, before, totals, sems = refs[19:]
    n = QROWS // ROWS
    out_copies = [
        pltpu.make_async_copy(totals.at[q], sums.at[pl.ds(q * n % NZ, n), q * n // NZ], sems.at[q]) for q in range(QUADS)
    ]
    step_id = pl.program_id(0)

    @pl.when(step_id == 0)
    def _():
        token = lambda dim: lax.broadcasted_iota(jnp.int32, (QROWS, QROWS), dim)
        before[...] = (token(0) < token(1)).astype(F32).astype(BF)

    @pl.when(step_id < QUADS)
    def _():
        expert = (pos[3] + lax.broadcasted_iota(jnp.int32, (8, 1), 0)).astype(F32)
        meta = [rows[i * ROWS : i * ROWS + META, 2 * WIDTH :].astype(F32) for i in range(QROWS // ROWS)]
        meta = jnp.concatenate(meta, axis=1)
        member = jnp.zeros((8, QROWS), F32)
        gates = jnp.zeros((8, QROWS), F32)
        for k in range(8):
            hit = meta[k : k + 1, :] == expert
            member = jnp.where(hit, 1.0, member)
            gates = jnp.where(hit, meta[8 + k : 9 + k, :], gates)
        slot = jnp.where(member > 0.0, dot(member.astype(BF), before[...], (1, 0)), -1.0)
        srow[step_id] = slot
        picks = pick_rows(slot)
        at = pl.ds(pl.multiple_of(step_id * QSLOTS, QSLOTS), QSLOTS)
        for half, to in enumerate((xg, gg)):
            to[:, at, :] = (
                dot(picks, rows[:, half * WIDTH : (half + 1) * WIDTH], (1, 0))
                .astype(BF)
                .reshape(EXPERTS_CORE, QSLOTS, WIDTH)
            )
        slot_gates = dot(picks, gates.astype(BF), (1, 1))
        for e in range(EXPERTS_CORE):
            weighting[e, at, :] = jnp.broadcast_to(
                slot_gates[e * QSLOTS : (e + 1) * QSLOTS, e : e + 1], (QSLOTS, 128)
            )

    @pl.when(step_id >= QUADS)
    def _():
        e = step_id - QUADS
        values = expert_step(pos, e, a_in, b_in, wg, wd, xg, gg, weighting, slot_grad)

        @pl.when(e == EXPERTS_CORE - 1)
        def _():
            for q in range(QUADS):
                total = dot(pick_rows(srow[q]), slot_grad[q], (0, 0)).astype(BF)
                totals[q] = total.reshape(n, ROWS, WIDTH)
                out_copies[q].start()

        for rows_in, value, out, y_first in zip((xg, gg), values, (a_out, b_out), (True, False)):
            term[...] = (dot(rows_in[e], value, (0, 0)) * scale).astype(BF)
            for k in range(4):
                for j in range(4):
                    piece = term[pl.ds(row_of(pos, *((k, j) if y_first else (j, k))), PIECE), :]
                    to, at = place(k, j)
                    out[to][at, 0] = piece

    @pl.when(step_id == QUADS + EXPERTS_CORE - 1)
    def _():
        for copy in out_copies:
            copy.wait()


def place(k, j):
    if k == 0:
        return 0, j
    if k == 1:
        return (3, j) if j < 2 else (1, j - 2)
    if k == 2:
        return (1, j + 2) if j < 2 else (2, j)
    return (2, j) if j < 2 else (4, j - 2)


def expert_step(pos, e, a_in, b_in, wg, wd, xg, gg, weighting, slot_grad):
    way = pos[4]
    for ky in range(NY):
        for kx in range(NX):
            at = pl.ds(row_of(pos, -way * ky, -way * kx), PIECE)
            wg[at, :] = a_in[ky][kx, 0]
            wd[at, :] = b_in[kx][ky, 0]
    gate = weighting[e][:, :1]
    pre = dot(xg[e], wg[...], (1, 0))
    hidden = dot(gg[e], wd[...], (1, 0))
    sigmoid = jax.nn.sigmoid(pre)
    scaled = (gate * (pre * sigmoid)).astype(BF)
    grad = (gate * hidden * (sigmoid * (1.0 + pre * (1.0 - sigmoid)))).astype(BF)
    back = dot(grad, wg[...], (1, 1)).astype(BF)
    for q in range(QUADS):
        slot_grad[q, pl.ds(pl.multiple_of(e * QSLOTS, QSLOTS), QSLOTS), :] = back[q * QSLOTS : (q + 1) * QSLOTS]
    return grad, scaled


def layer(scale, pos, rows, a_in, b_in):
    expert = lambda i: jnp.maximum(i - QUADS, 0)
    piece = lambda n: pl.BlockSpec((n, 1, PIECE, HID), lambda i, p: (0, expert(i), 0, 0))
    grads = lambda n, near: (pltpu.VMEM if near else jax.ShapeDtypeStruct)((n, EXPERTS_CORE, PIECE, HID), BF)
    by_z = (NZ, NC, ROWS, WIDTH)
    slots = lambda n, dtype: pltpu.VMEM((EXPERTS_CORE, SLOTS, n), dtype)
    out = pl.pallas_call(
        lambda *refs: layer_kernel(scale, *refs),
        grid_spec=pltpu.PrefetchScalarGridSpec(
            num_scalar_prefetch=1,
            grid=(QUADS + EXPERTS_CORE,),
            in_specs=[pl.BlockSpec((QROWS, rows.shape[1]), lambda i, p: (jnp.minimum(i, QUADS - 1), 0))]
            + [piece(4)] * 8,
            out_specs=[ANYWHERE] + [piece(n) for n in PARTS * 2],
            scratch_shapes=[pltpu.VMEM((WIDTH, HID), BF)] * 3
            + [slots(WIDTH, BF), slots(WIDTH, BF), slots(128, F32)]
            + [pltpu.VMEM((QUADS, EXPERTS_CORE * QSLOTS, WIDTH), BF), pltpu.VMEM((QUADS, 8, QROWS), F32)]
            + [pltpu.VMEM((QROWS, QROWS), BF), pltpu.VMEM((QUADS, QROWS // ROWS, ROWS, WIDTH), BF)]
            + [pltpu.SemaphoreType.DMA((QUADS,))],
        ),
        out_shape=[jax.ShapeDtypeStruct(by_z, BF)] + [grads(n, i % 5 in (0, 3, 4)) for i, n in enumerate(PARTS * 2)],
        compiler_params=PARAMS,
        cost_estimate=cost(13_000_000_000, 26_000_000, 600_000),
    )(pos, rows, *a_in, *b_in)
    return out[0], out[1:6], out[6:11]


def gather_plane(own, first, second):
    plane = [jnp.stack([own] + [step(own, first, k) for k in range(1, SIZES[first])])]
    for _ in range(SIZES[second] - 1):
        plane.append(step(plane[-1], second))
    return plane


def scatter_plane(parts, first, second):
    f32 = lambda a: a.astype(F32)
    own, up, down, next_up, next_down = parts
    up, down = shift(up, second, 1), shift(down, second, -1)
    n = own.shape[0] // 2
    next_up = shift((f32(next_up) + f32(up[n:])).astype(BF), second, 1)
    next_down = shift((f32(next_down) + f32(down[n:])).astype(BF), second, -1)
    low = f32(own[:n]) + f32(next_up) + f32(down[:n])
    high = f32(own[n:]) + f32(up[:n]) + f32(next_down)
    line = [half[i] for half in (low, high) for i in range(n)]
    return sum([line[0]] + [f32(shift(line[k].astype(BF), first, k)) for k in range(1, SIZES[first])])


def shards(tokens, out_grad, expert_ids, gate_values, gate_weight, down_weight):
    scale = 1.0 / math.sqrt(NY * NX * NC * NZ * ROWS * 8 / 64)
    y, x, c, z = (lax.axis_index(a) for a in ("y", "x", "c", "z"))
    pos = jnp.stack([y, x, c, (z * NC + c) * EXPERTS_CORE, 1 - 2 * c]).astype(jnp.int32)
    ids = jnp.pad(expert_ids.T.astype(BF), ((0, ROWS - META // 2), (0, 0)))
    gates = jnp.pad(gate_values.T, ((META // 2, ROWS - META), (0, 0)))
    meta = jnp.maximum(ids, gates)
    rows = lax.all_gather(jnp.concatenate([tokens, out_grad, meta], axis=1), ("c", "z"), axis=0, tiled=True)

    def by_core(own, sister):
        return jnp.where(c == 0, own, sister), jnp.where(c == 0, sister, own)

    def halves(weight):
        rows = weight.transpose(1, 0, 2).reshape(NC, EXPERTS_CORE, weight.shape[0], HID)
        return by_core(rows[0], rows[1])

    (keep_a, send_a), (keep_b, send_b) = halves(gate_weight), halves(down_weight)
    got = swap(jnp.stack([send_a, send_b]))
    own_a = jnp.concatenate(by_core(keep_a, got[0]), axis=1)
    own_b = jnp.concatenate(by_core(keep_b, got[1]), axis=1)
    a_in = gather_plane(own_a, "x", "y")
    b_in = gather_plane(own_b, "y", "x")
    sums, a_out, b_out = layer(scale, pos, rows, a_in, b_in)
    part = lax.psum_scatter(sums, "z", scatter_dimension=0)
    got = swap(part)
    input_grad = jnp.where(c == 0, part[0].astype(F32) + got[0].astype(F32), part[1].astype(F32) + got[1].astype(F32)).astype(BF)

    def placed(total):
        n = gate_weight.shape[0]
        keep, send = by_core(total[:, :n], total[:, n:])
        both = by_core(keep, swap(send.astype(BF)).astype(F32))
        return jnp.concatenate(both).transpose(1, 0, 2)

    return input_grad, placed(scatter_plane(a_out, "x", "y")), placed(scatter_plane(b_out, "y", "x"))


def solution(mesh):
    fine = Mesh(mesh.devices.reshape(NY, NX, NC, NZ), ("y", "x", "c", "z"))
    rows = P(("y", "x", "c", "z"), None)
    weights = P(("y", "x", "c"), "z", None)
    return jax.shard_map(
        shards,
        mesh=fine,
        in_specs=(rows, rows, rows, rows, weights, weights),
        out_specs=(rows, weights, weights),
        check_vma=False,
    )
```

```python
import math

import jax
import jax.numpy as jnp
from jax import lax
from jax.experimental import pallas as pl
from jax.experimental.pallas import tpu as pltpu
from jax.sharding import Mesh
from jax.sharding import PartitionSpec as P

BF, F32 = jnp.bfloat16, jnp.float32
NY, NX, NC, NZ = 4, 4, 2, 8
ROWS, WIDTH, HID = 128, 1024, 384
EXPERTS_CORE = 4
META = 16
CAP = 20
QROWS = 4 * ROWS
QSLOTS = 4 * CAP
QUADS = NC * NZ * ROWS // QROWS
SLOTS = QUADS * QSLOTS
PIECE = WIDTH // (NY * NX)
PARTS = (4, 4, 4, 2, 2)
SIZES = {"y": NY, "x": NX}
ANYWHERE = pl.BlockSpec(memory_space=pl.ANY)
PARAMS = pltpu.CompilerParams(vmem_limit_bytes=54 * 2**20)


def swap(value):
    return lax.ppermute(value, "c", [(0, 1), (1, 0)])


def step(value, axis, by=1):
    n = SIZES[axis]
    pairs = [(2 * i + c, 2 * ((i + by * (1 - 2 * c)) % n) + c) for i in range(n) for c in range(NC)]
    return lax.ppermute(value, (axis, "c"), pairs)


def shift(value, axis, by):
    n = SIZES[axis]
    return lax.ppermute(value, axis, [(i, (i + by) % n) for i in range(n)])


def dot(a, b, contract):
    return lax.dot_general(a, b, ((contract[:1], contract[1:]), ((), ())), preferred_element_type=F32)


def cost(flops, moved, other=0):
    return pl.CostEstimate(flops=flops, bytes_accessed=moved, transcendentals=other)


def row_of(pos, ky, kx):
    y, x = (pos[0] + ky) & (NY - 1), (pos[1] + kx) & (NX - 1)
    return pl.multiple_of((y * NX + x) * PIECE, PIECE)


def pick_rows(srow):
    iota = lax.broadcasted_iota(jnp.int32, (QSLOTS, QROWS), 0).astype(F32)
    picks = [(srow[e : e + 1, :] == iota).astype(F32).astype(BF) for e in range(EXPERTS_CORE)]
    return jnp.concatenate(picks, axis=0)


def layer_kernel(scale, pos, rows, *refs):
    a_in, b_in = refs[0:4], refs[4:8]
    sums, a_out, gg_out, scaled_out = refs[8], refs[9:14], refs[14], refs[15]
    wg, wd, term, xg, gg, weighting, slot_grad, srow, before, totals, sems = refs[16:]
    n = QROWS // ROWS
    out_copies = [
        pltpu.make_async_copy(totals.at[q], sums.at[pl.ds(q * n % NZ, n), q * n // NZ], sems.at[q]) for q in range(QUADS)
    ]
    step_id = pl.program_id(0)

    @pl.when(step_id == 0)
    def _():
        token = lambda dim: lax.broadcasted_iota(jnp.int32, (QROWS, QROWS), dim)
        before[...] = (token(0) < token(1)).astype(F32).astype(BF)

    @pl.when(step_id < QUADS)
    def _():
        expert = (pos[3] + lax.broadcasted_iota(jnp.int32, (8, 1), 0)).astype(F32)
        meta = [rows[i * ROWS : i * ROWS + META, 2 * WIDTH :].astype(F32) for i in range(QROWS // ROWS)]
        meta = jnp.concatenate(meta, axis=1)
        member = jnp.zeros((8, QROWS), F32)
        gates = jnp.zeros((8, QROWS), F32)
        for k in range(8):
            hit = meta[k : k + 1, :] == expert
            member = jnp.where(hit, 1.0, member)
            gates = jnp.where(hit, meta[8 + k : 9 + k, :], gates)
        slot = jnp.where(member > 0.0, dot(member.astype(BF), before[...], (1, 0)), -1.0)
        srow[step_id] = slot
        picks = pick_rows(slot)
        at = pl.ds(pl.multiple_of(step_id * QSLOTS, QSLOTS), QSLOTS)
        for half, to in enumerate((xg, gg)):
            to[:, at, :] = (
                dot(picks, rows[:, half * WIDTH : (half + 1) * WIDTH], (1, 0))
                .astype(BF)
                .reshape(EXPERTS_CORE, QSLOTS, WIDTH)
            )
        slot_gates = dot(picks, gates.astype(BF), (1, 1))
        for e in range(EXPERTS_CORE):
            weighting[e, at, :] = jnp.broadcast_to(
                slot_gates[e * QSLOTS : (e + 1) * QSLOTS, e : e + 1], (QSLOTS, 128)
            )

    @pl.when(step_id >= QUADS)
    def _():
        e = step_id - QUADS
        grad, scaled = expert_step(pos, e, a_in, b_in, wg, wd, xg, gg, weighting, slot_grad)

        @pl.when(e == EXPERTS_CORE - 1)
        def _():
            for q in range(QUADS):
                total = dot(pick_rows(srow[q]), slot_grad[q], (0, 0)).astype(BF)
                totals[q] = total.reshape(n, ROWS, WIDTH)
                out_copies[q].start()

        gg_out[0] = gg[e]
        scaled_out[0] = scaled
        write_terms(scale, pos, xg[e], grad, a_out, term, True)

    @pl.when(step_id == QUADS + EXPERTS_CORE - 1)
    def _():
        for copy in out_copies:
            copy.wait()


def write_terms(scale, pos, rows, value, out, term, y_first):
    term[...] = (dot(rows, value, (0, 0)) * scale).astype(BF)
    for k in range(4):
        for j in range(4):
            piece = term[pl.ds(row_of(pos, *((k, j) if y_first else (j, k))), PIECE), :]
            to, at = place(k, j)
            out[to][at, 0] = piece


def down_kernel(scale, pos, gg, scaled, *refs):
    write_terms(scale, pos, gg[0], scaled[0], refs[:5], refs[5], False)


def grads_of(i):
    kind = pltpu.VMEM if i in (0, 3, 4) else jax.ShapeDtypeStruct
    return kind((PARTS[i], EXPERTS_CORE, PIECE, HID), BF)


def down_terms(scale, pos, gg, scaled):
    slots = lambda n: pl.BlockSpec((1, SLOTS, n), lambda e, p: (e, 0, 0))
    return pl.pallas_call(
        lambda *refs: down_kernel(scale, *refs),
        grid_spec=pltpu.PrefetchScalarGridSpec(
            num_scalar_prefetch=1,
            grid=(EXPERTS_CORE,),
            in_specs=[slots(WIDTH), slots(HID)],
            out_specs=[pl.BlockSpec((n, 1, PIECE, HID), lambda e, p: (0, e, 0, 0)) for n in PARTS],
            scratch_shapes=[pltpu.VMEM((WIDTH, HID), BF)],
        ),
        out_shape=[grads_of(i) for i in range(5)],
        compiler_params=PARAMS,
        cost_estimate=cost(2_000_000_000, 7_000_000),
    )(pos, gg, scaled)


def place(k, j):
    if k == 0:
        return 0, j
    if k == 1:
        return (3, j) if j < 2 else (1, j - 2)
    if k == 2:
        return (1, j + 2) if j < 2 else (2, j)
    return (2, j) if j < 2 else (4, j - 2)


def expert_step(pos, e, a_in, b_in, wg, wd, xg, gg, weighting, slot_grad):
    way = pos[4]
    for ky in range(NY):
        for kx in range(NX):
            at = pl.ds(row_of(pos, -way * ky, -way * kx), PIECE)
            wg[at, :] = a_in[ky][kx, 0]
            wd[at, :] = b_in[kx][ky, 0]
    gate = weighting[e][:, :1]
    pre = dot(xg[e], wg[...], (1, 0))
    hidden = dot(gg[e], wd[...], (1, 0))
    sigmoid = jax.nn.sigmoid(pre)
    scaled = (gate * (pre * sigmoid)).astype(BF)
    grad = (gate * hidden * (sigmoid * (1.0 + pre * (1.0 - sigmoid)))).astype(BF)
    back = dot(grad, wg[...], (1, 1)).astype(BF)
    for q in range(QUADS):
        slot_grad[q, pl.ds(pl.multiple_of(e * QSLOTS, QSLOTS), QSLOTS), :] = back[q * QSLOTS : (q + 1) * QSLOTS]
    return grad, scaled


def layer(scale, pos, rows, a_in, b_in):
    expert = lambda i: jnp.maximum(i - QUADS, 0)
    piece = lambda n: pl.BlockSpec((n, 1, PIECE, HID), lambda i, p: (0, expert(i), 0, 0))
    slots_out = lambda n: pl.BlockSpec((1, SLOTS, n), lambda i, p: (expert(i), 0, 0))
    by_z = (NZ, NC, ROWS, WIDTH)
    slots = lambda n, dtype: pltpu.VMEM((EXPERTS_CORE, SLOTS, n), dtype)
    out = pl.pallas_call(
        lambda *refs: layer_kernel(scale, *refs),
        grid_spec=pltpu.PrefetchScalarGridSpec(
            num_scalar_prefetch=1,
            grid=(QUADS + EXPERTS_CORE,),
            in_specs=[pl.BlockSpec((QROWS, rows.shape[1]), lambda i, p: (jnp.minimum(i, QUADS - 1), 0))]
            + [piece(4)] * 8,
            out_specs=[ANYWHERE] + [piece(n) for n in PARTS] + [slots_out(WIDTH), slots_out(HID)],
            scratch_shapes=[pltpu.VMEM((WIDTH, HID), BF)] * 3
            + [slots(WIDTH, BF), slots(WIDTH, BF), slots(128, F32)]
            + [pltpu.VMEM((QUADS, EXPERTS_CORE * QSLOTS, WIDTH), BF), pltpu.VMEM((QUADS, 8, QROWS), F32)]
            + [pltpu.VMEM((QROWS, QROWS), BF), pltpu.VMEM((QUADS, QROWS // ROWS, ROWS, WIDTH), BF)]
            + [pltpu.SemaphoreType.DMA((QUADS,))],
        ),
        out_shape=[jax.ShapeDtypeStruct(by_z, BF)] + [grads_of(i) for i in range(5)]
        + [jax.ShapeDtypeStruct((EXPERTS_CORE, SLOTS, n), BF) for n in (WIDTH, HID)],
        compiler_params=PARAMS,
        cost_estimate=cost(13_000_000_000, 26_000_000, 600_000),
    )(pos, rows, *a_in, *b_in)
    return out[0], out[1:6], out[6], out[7]


def gather_plane(own, first, second):
    plane = [jnp.stack([own] + [step(own, first, k) for k in range(1, SIZES[first])])]
    for _ in range(SIZES[second] - 1):
        plane.append(step(plane[-1], second))
    return plane


def scatter_plane(parts, first, second):
    f32 = lambda a: a.astype(F32)
    own, up, down, next_up, next_down = parts
    up, down = shift(up, second, 1), shift(down, second, -1)
    n = own.shape[0] // 2
    next_up = shift((f32(next_up) + f32(up[n:])).astype(BF), second, 1)
    next_down = shift((f32(next_down) + f32(down[n:])).astype(BF), second, -1)
    low = f32(own[:n]) + f32(next_up) + f32(down[:n])
    high = f32(own[n:]) + f32(up[:n]) + f32(next_down)
    line = [half[i] for half in (low, high) for i in range(n)]
    return sum([line[0]] + [f32(shift(line[k].astype(BF), first, k)) for k in range(1, SIZES[first])])


def shards(tokens, out_grad, expert_ids, gate_values, gate_weight, down_weight):
    scale = 1.0 / math.sqrt(NY * NX * NC * NZ * ROWS * 8 / 64)
    y, x, c, z = (lax.axis_index(a) for a in ("y", "x", "c", "z"))
    pos = jnp.stack([y, x, c, (z * NC + c) * EXPERTS_CORE, 1 - 2 * c]).astype(jnp.int32)
    ids = jnp.pad(expert_ids.T.astype(BF), ((0, ROWS - META // 2), (0, 0)))
    gates = jnp.pad(gate_values.T, ((META // 2, ROWS - META), (0, 0)))
    meta = jnp.maximum(ids, gates)
    rows = lax.all_gather(jnp.concatenate([tokens, out_grad, meta], axis=1), ("c", "z"), axis=0, tiled=True)

    def by_core(own, sister):
        return jnp.where(c == 0, own, sister), jnp.where(c == 0, sister, own)

    def halves(weight):
        rows = weight.transpose(1, 0, 2).reshape(NC, EXPERTS_CORE, weight.shape[0], HID)
        return by_core(rows[0], rows[1])

    (keep_a, send_a), (keep_b, send_b) = halves(gate_weight), halves(down_weight)
    got = swap(jnp.stack([send_a, send_b]))
    own_a = jnp.concatenate(by_core(keep_a, got[0]), axis=1)
    own_b = jnp.concatenate(by_core(keep_b, got[1]), axis=1)
    a_in = gather_plane(own_a, "x", "y")
    b_in = gather_plane(own_b, "y", "x")
    sums, a_out, gg, scaled = layer(scale, pos, rows, a_in, b_in)
    b_out = down_terms(scale, pos, gg, scaled)
    part = lax.psum_scatter(sums, "z", scatter_dimension=0)
    got = swap(part)
    input_grad = jnp.where(c == 0, part[0].astype(F32) + got[0].astype(F32), part[1].astype(F32) + got[1].astype(F32)).astype(BF)

    def placed(total):
        n = gate_weight.shape[0]
        keep, send = by_core(total[:, :n], total[:, n:])
        both = by_core(keep, swap(send.astype(BF)).astype(F32))
        return jnp.concatenate(both).transpose(1, 0, 2)

    return input_grad, placed(scatter_plane(a_out, "x", "y")), placed(scatter_plane(b_out, "y", "x"))


def solution(mesh):
    fine = Mesh(mesh.devices.reshape(NY, NX, NC, NZ), ("y", "x", "c", "z"))
    rows = P(("y", "x", "c", "z"), None)
    weights = P(("y", "x", "c"), "z", None)
    return jax.shard_map(
        shards,
        mesh=fine,
        in_specs=(rows, rows, rows, rows, weights, weights),
        out_specs=(rows, weights, weights),
        check_vma=False,
    )
```

```python
import math

import jax
import jax.numpy as jnp
from jax import lax
from jax.experimental import pallas as pl
from jax.experimental.pallas import tpu as pltpu
from jax.sharding import Mesh
from jax.sharding import PartitionSpec as P

BF, F32 = jnp.bfloat16, jnp.float32
NY, NX, NC, NZ = 4, 4, 2, 8
ROWS, WIDTH, HID = 128, 1024, 384
EXPERTS_CORE = 4
META = 16
CAP = 20
QROWS = 4 * ROWS
QSLOTS = 4 * CAP
QUADS = NC * NZ * ROWS // QROWS
SLOTS = QUADS * QSLOTS
PIECE = WIDTH // (NY * NX)
PARTS = (4, 4, 4, 2, 2)
SIZES = {"y": NY, "x": NX}
ANYWHERE = pl.BlockSpec(memory_space=pl.ANY)
PARAMS = pltpu.CompilerParams(vmem_limit_bytes=54 * 2**20)


def swap(value):
    return lax.ppermute(value, "c", [(0, 1), (1, 0)])


def step(value, axis, by=1):
    n = SIZES[axis]
    pairs = [(2 * i + c, 2 * ((i + by * (1 - 2 * c)) % n) + c) for i in range(n) for c in range(NC)]
    return lax.ppermute(value, (axis, "c"), pairs)


def shift(value, axis, by):
    n = SIZES[axis]
    return lax.ppermute(value, axis, [(i, (i + by) % n) for i in range(n)])


def dot(a, b, contract):
    return lax.dot_general(a, b, ((contract[:1], contract[1:]), ((), ())), preferred_element_type=F32)


def cost(flops, moved, other=0):
    return pl.CostEstimate(flops=flops, bytes_accessed=moved, transcendentals=other)


def row_of(pos, ky, kx):
    y, x = (pos[0] + ky) & (NY - 1), (pos[1] + kx) & (NX - 1)
    return pl.multiple_of((y * NX + x) * PIECE, PIECE)


def pick_rows(srow):
    iota = lax.broadcasted_iota(jnp.int32, (QSLOTS, QROWS), 0).astype(F32)
    picks = [(srow[e : e + 1, :] == iota).astype(F32).astype(BF) for e in range(EXPERTS_CORE)]
    return jnp.concatenate(picks, axis=0)


def layer_kernel(scale, pos, rows, *refs):
    a_in, b_in = refs[0:4], refs[4:8]
    sums, a_out, b_out = refs[8], refs[9:14], refs[14:19]
    wg, wd, term, xg, gg, weighting, slot_grad, kept, before, totals, sems = refs[19:]
    n = QROWS // ROWS
    out_copies = [
        pltpu.make_async_copy(totals.at[q], sums.at[pl.ds(q * n % NZ, n), q * n // NZ], sems.at[q]) for q in range(QUADS)
    ]
    step_id = pl.program_id(0)

    @pl.when(step_id == 0)
    def _():
        token = lambda dim: lax.broadcasted_iota(jnp.int32, (QROWS, QROWS), dim)
        before[...] = (token(0) < token(1)).astype(F32).astype(BF)

    @pl.when(step_id < QUADS)
    def _():
        expert = (pos[3] + lax.broadcasted_iota(jnp.int32, (8, 1), 0)).astype(F32)
        meta = [rows[i * ROWS : i * ROWS + META, 2 * WIDTH :].astype(F32) for i in range(QROWS // ROWS)]
        meta = jnp.concatenate(meta, axis=1)
        member = jnp.zeros((8, QROWS), F32)
        gates = jnp.zeros((8, QROWS), F32)
        for k in range(8):
            hit = meta[k : k + 1, :] == expert
            member = jnp.where(hit, 1.0, member)
            gates = jnp.where(hit, meta[8 + k : 9 + k, :], gates)
        slot = jnp.where(member > 0.0, dot(member.astype(BF), before[...], (1, 0)), -1.0)
        picks = pick_rows(slot)
        kept[step_id] = picks
        at = pl.ds(pl.multiple_of(step_id * QSLOTS, QSLOTS), QSLOTS)
        for half, to in enumerate((xg, gg)):
            to[:, at, :] = (
                dot(picks, rows[:, half * WIDTH : (half + 1) * WIDTH], (1, 0))
                .astype(BF)
                .reshape(EXPERTS_CORE, QSLOTS, WIDTH)
            )
        slot_gates = dot(picks, gates.astype(BF), (1, 1))
        for e in range(EXPERTS_CORE):
            weighting[e, at, :] = jnp.broadcast_to(
                slot_gates[e * QSLOTS : (e + 1) * QSLOTS, e : e + 1], (QSLOTS, 128)
            )

    @pl.when(step_id >= QUADS)
    def _():
        e = step_id - QUADS
        values = expert_step(pos, e, a_in, b_in, wg, wd, xg, gg, weighting, slot_grad)

        @pl.when(e == EXPERTS_CORE - 1)
        def _():
            for q in range(QUADS):
                total = dot(kept[q], slot_grad[q], (0, 0)).astype(BF)
                totals[q] = total.reshape(n, ROWS, WIDTH)
                out_copies[q].start()

        for rows_in, value, out, y_first in zip((xg, gg), values, (a_out, b_out), (True, False)):
            term[...] = (dot(rows_in[e], value, (0, 0)) * scale).astype(BF)
            for k in range(4):
                for j in range(4):
                    piece = term[pl.ds(row_of(pos, *((k, j) if y_first else (j, k))), PIECE), :]
                    to, at = place(k, j)
                    out[to][at, 0] = piece

    @pl.when(step_id == QUADS + EXPERTS_CORE - 1)
    def _():
        for copy in out_copies:
            copy.wait()


def place(k, j):
    if k == 0:
        return 0, j
    if k == 1:
        return (3, j) if j < 2 else (1, j - 2)
    if k == 2:
        return (1, j + 2) if j < 2 else (2, j)
    return (2, j) if j < 2 else (4, j - 2)


def expert_step(pos, e, a_in, b_in, wg, wd, xg, gg, weighting, slot_grad):
    way = pos[4]
    for ky in range(NY):
        for kx in range(NX):
            at = pl.ds(row_of(pos, -way * ky, -way * kx), PIECE)
            wg[at, :] = a_in[ky][kx, 0]
            wd[at, :] = b_in[kx][ky, 0]
    gate = weighting[e][:, :1]
    pre = dot(xg[e], wg[...], (1, 0))
    hidden = dot(gg[e], wd[...], (1, 0))
    sigmoid = jax.nn.sigmoid(pre)
    scaled = (gate * (pre * sigmoid)).astype(BF)
    grad = (gate * hidden * (sigmoid * (1.0 + pre * (1.0 - sigmoid)))).astype(BF)
    back = dot(grad, wg[...], (1, 1)).astype(BF)
    for q in range(QUADS):
        slot_grad[q, pl.ds(pl.multiple_of(e * QSLOTS, QSLOTS), QSLOTS), :] = back[q * QSLOTS : (q + 1) * QSLOTS]
    return grad, scaled


def layer(scale, pos, rows, a_in, b_in):
    expert = lambda i: jnp.maximum(i - QUADS, 0)
    piece = lambda n: pl.BlockSpec((n, 1, PIECE, HID), lambda i, p: (0, expert(i), 0, 0))
    grads = lambda n, near: (pltpu.VMEM if near else jax.ShapeDtypeStruct)((n, EXPERTS_CORE, PIECE, HID), BF)
    by_z = (NZ, NC, ROWS, WIDTH)
    slots = lambda n, dtype: pltpu.VMEM((EXPERTS_CORE, SLOTS, n), dtype)
    out = pl.pallas_call(
        lambda *refs: layer_kernel(scale, *refs),
        grid_spec=pltpu.PrefetchScalarGridSpec(
            num_scalar_prefetch=1,
            grid=(QUADS + EXPERTS_CORE,),
            in_specs=[pl.BlockSpec((QROWS, rows.shape[1]), lambda i, p: (jnp.minimum(i, QUADS - 1), 0))]
            + [piece(4)] * 8,
            out_specs=[ANYWHERE] + [piece(n) for n in PARTS * 2],
            scratch_shapes=[pltpu.VMEM((WIDTH, HID), BF)] * 3
            + [slots(WIDTH, BF), slots(WIDTH, BF), slots(128, F32)]
            + [pltpu.VMEM((QUADS, EXPERTS_CORE * QSLOTS, WIDTH), BF), pltpu.VMEM((QUADS, EXPERTS_CORE * QSLOTS, QROWS), BF)]
            + [pltpu.VMEM((QROWS, QROWS), BF), pltpu.VMEM((QUADS, QROWS // ROWS, ROWS, WIDTH), BF)]
            + [pltpu.SemaphoreType.DMA((QUADS,))],
        ),
        out_shape=[jax.ShapeDtypeStruct(by_z, BF)] + [grads(n, i % 5 in (0, 3, 4)) for i, n in enumerate(PARTS * 2)],
        compiler_params=PARAMS,
        cost_estimate=cost(13_000_000_000, 26_000_000, 600_000),
    )(pos, rows, *a_in, *b_in)
    return out[0], out[1:6], out[6:11]


def gather_plane(own, first, second):
    plane = [jnp.stack([own] + [step(own, first, k) for k in range(1, SIZES[first])])]
    for _ in range(SIZES[second] - 1):
        plane.append(step(plane[-1], second))
    return plane


def scatter_plane(parts, first, second):
    f32 = lambda a: a.astype(F32)
    own, up, down, next_up, next_down = parts
    up, down = shift(up, second, 1), shift(down, second, -1)
    n = own.shape[0] // 2
    next_up = shift((f32(next_up) + f32(up[n:])).astype(BF), second, 1)
    next_down = shift((f32(next_down) + f32(down[n:])).astype(BF), second, -1)
    low = f32(own[:n]) + f32(next_up) + f32(down[:n])
    high = f32(own[n:]) + f32(up[:n]) + f32(next_down)
    line = [half[i] for half in (low, high) for i in range(n)]
    return sum([line[0]] + [f32(shift(line[k].astype(BF), first, k)) for k in range(1, SIZES[first])])


def shards(tokens, out_grad, expert_ids, gate_values, gate_weight, down_weight):
    scale = 1.0 / math.sqrt(NY * NX * NC * NZ * ROWS * 8 / 64)
    y, x, c, z = (lax.axis_index(a) for a in ("y", "x", "c", "z"))
    pos = jnp.stack([y, x, c, (z * NC + c) * EXPERTS_CORE, 1 - 2 * c]).astype(jnp.int32)
    ids = jnp.pad(expert_ids.T.astype(BF), ((0, ROWS - META // 2), (0, 0)))
    gates = jnp.pad(gate_values.T, ((META // 2, ROWS - META), (0, 0)))
    meta = jnp.maximum(ids, gates)
    rows = lax.all_gather(jnp.concatenate([tokens, out_grad, meta], axis=1), ("c", "z"), axis=0, tiled=True)

    def by_core(own, sister):
        return jnp.where(c == 0, own, sister), jnp.where(c == 0, sister, own)

    def halves(weight):
        rows = weight.transpose(1, 0, 2).reshape(NC, EXPERTS_CORE, weight.shape[0], HID)
        return by_core(rows[0], rows[1])

    (keep_a, send_a), (keep_b, send_b) = halves(gate_weight), halves(down_weight)
    got = swap(jnp.stack([send_a, send_b]))
    own_a = jnp.concatenate(by_core(keep_a, got[0]), axis=1)
    own_b = jnp.concatenate(by_core(keep_b, got[1]), axis=1)
    a_in = gather_plane(own_a, "x", "y")
    b_in = gather_plane(own_b, "y", "x")
    sums, a_out, b_out = layer(scale, pos, rows, a_in, b_in)
    part = lax.psum_scatter(sums, "z", scatter_dimension=0)
    got = swap(part)
    input_grad = jnp.where(c == 0, part[0].astype(F32) + got[0].astype(F32), part[1].astype(F32) + got[1].astype(F32)).astype(BF)

    def placed(total):
        n = gate_weight.shape[0]
        keep, send = by_core(total[:, :n], total[:, n:])
        both = by_core(keep, swap(send.astype(BF)).astype(F32))
        return jnp.concatenate(both).transpose(1, 0, 2)

    return input_grad, placed(scatter_plane(a_out, "x", "y")), placed(scatter_plane(b_out, "y", "x"))


def solution(mesh):
    fine = Mesh(mesh.devices.reshape(NY, NX, NC, NZ), ("y", "x", "c", "z"))
    rows = P(("y", "x", "c", "z"), None)
    weights = P(("y", "x", "c"), "z", None)
    return jax.shard_map(
        shards,
        mesh=fine,
        in_specs=(rows, rows, rows, rows, weights, weights),
        out_specs=(rows, weights, weights),
        check_vma=False,
    )
```
